512 devices in a mesh: ctx: 64 (over z, x, core), kvh: 8 (over y).
Axes of the slice: x: 4, y: 8, z: 8, core: 2. Of those that a mesh axis runs over, the one named last changes fastest.
Arguments:
- query_states: bfloat16 [24576, 4096], P('ctx', 'kvh')
- key_states: bfloat16 [24576, 1024], P('ctx', 'kvh')
- value_states: bfloat16 [24576, 1024], P('ctx', 'kvh'), may hold values from -6 to 6
- grad_output: bfloat16 [24576, 4096], P(('ctx', 'kvh')), may hold values from -6 to 6
- doc_start: int32 [192], P('ctx'), may hold values from 0 to 23424, as said below
Outputs:
- grad_query: bfloat16 [24576, 4096], P(('ctx', 'kvh'))
- grad_key: bfloat16 [24576, 1024], P('ctx', 'kvh')
- grad_value: bfloat16 [24576, 1024], P('ctx', 'kvh')
The draws below stay inside these ranges and needn't reach their ends.
Inputs may be any that keep to these rules, and one draw needn't show every extreme that they name: Documents are whole runs of blocks; doc_start is the same for all blocks of one document and equals the position of its first block. Every document has at most 1152 tokens, and the last 1152 tokens of the sequence form one document.
All inputs are finite; a program needn't handle non-finite values.
Results may differ from the reference program's by a relative error of at most 0.03.
Values may be sent and summed in bfloat16 or wider, within the bound.
No kernel may reach another device: no remote copies, remote signals or barrier semaphores. Data moves between devices by JAX's collectives and lax.ppermute only.
A program may use at most 64 MiB of HBM per device.

```python
import jax
import jax.numpy as jnp
from jax import lax

HD = 128
QPK = 4
TOK_DEV = 384
BLK = 128
SPAN = 4
KVH = 8
HEADS = 32
TOKENS = 24576
MAXDOC = 1152
NBLK = 192
N_CTX = 64


def shared_keys(key):
    base = jax.random.normal(key, (TOKENS, KVH * HD), jnp.float32)
    return jnp.clip(base, -6.0, 6.0)


def draw_key_states(key, part):
    base = shared_keys(key)
    return base.astype(jnp.bfloat16)


def draw_query_states(key, part):
    key = jax.random.fold_in(key, 5)
    own = jnp.clip(jax.random.normal(key, (TOKENS, HEADS * HD), jnp.float32), -6.0, 6.0)
    return own.astype(jnp.bfloat16)


def draw_doc_start(key, part):
    key = jax.random.fold_in(key, 11)
    blocks_most = MAXDOC // BLK
    key_short, key_long, key_pick, key_place = jax.random.split(key, 4)
    short_len = jax.random.randint(key_short, (NBLK,), 1, 3, jnp.int32)
    long_len = jax.random.randint(key_long, (NBLK,), max(blocks_most // 2, 1), blocks_most + 1, jnp.int32)
    picked = jax.random.randint(key_pick, (NBLK,), 0, 2, jnp.int32)
    lengths = jnp.where(picked == 1, long_len, short_len)
    placed = jax.random.randint(key_place, (), 0, 2, jnp.int32)
    lengths = jnp.where(jnp.arange(NBLK, dtype=jnp.int32) == placed, blocks_most, lengths)
    firsts = jnp.concatenate([jnp.zeros((1,), jnp.int32), jnp.cumsum(lengths)[:-1].astype(jnp.int32)])
    marked = jnp.zeros((NBLK,), jnp.int32).at[firsts].set(firsts, mode='drop')
    last_first = NBLK - blocks_most
    marked = marked.at[last_first].set(last_first)
    running = lax.cummax(marked)
    block_index = jnp.arange(NBLK, dtype=jnp.int32)
    running = jnp.where(block_index >= last_first, last_first, running)
    return (running * BLK).astype(jnp.int32)


def block_scale(rng, dims, cuts, least, high):
    factor_of, own = 1.0, jax.random.fold_in(rng, 6)
    for position, shards_of in cuts:
        heights = jnp.exp(jax.random.uniform(jax.random.fold_in(own, position), (shards_of,), jnp.float32, least / len(cuts), high / len(cuts)))
        factor_of = factor_of * jnp.repeat(heights, dims[position] // shards_of).reshape([-1 if axis == position else 1 for axis in range(len(dims))])
    return factor_of


def normal_values(key, dims, scale, limit, cuts=(), kind=jnp.bfloat16):
    factor_of = block_scale(key, dims, cuts, -0.22, 0.18) if cuts else 1.0
    drawn = jax.random.normal(key, dims, jnp.float32) * scale * factor_of
    return jnp.minimum(jnp.maximum(drawn, -limit), limit).astype(kind)


def setup_inputs(seed: int = 0) -> dict:
    arg_keys = jax.random.split(jax.random.key(seed), 6)
    return {
        "query_states": draw_query_states(jax.random.fold_in(arg_keys[5], 71), 0),
        "key_states": draw_key_states(jax.random.fold_in(arg_keys[5], 71), 0),
        "value_states": normal_values(arg_keys[2], (TOKENS, KVH * HD), 1.0, 6.0, ((0, 64), (1, 8))),
        "grad_output": normal_values(arg_keys[3], (TOKENS, HEADS * HD), 1.0, 6.0, ((0, 512),)),
        "doc_start": draw_doc_start(jax.random.fold_in(arg_keys[5], 71), 0),
    }


masked_score = -1.0e30


def reference(query_states, key_states, value_states, grad_output, doc_start):
    inv_root = HD ** -0.5
    window = SPAN * TOK_DEV
    leading = (SPAN - 1) * TOK_DEV
    key_padded = jnp.concatenate([jnp.zeros((leading, KVH * HD), key_states.dtype), key_states], axis=0)
    value_padded = jnp.concatenate([jnp.zeros((leading, KVH * HD), value_states.dtype), value_states], axis=0)
    starts = jnp.repeat(doc_start, BLK)

    def one_span(carry, index_blk):
        key_acc, value_acc = carry
        first_row = (index_blk * TOK_DEV).astype(jnp.int32)
        query_blk = lax.dynamic_slice_in_dim(query_states, first_row, TOK_DEV, 0).astype(jnp.float32).reshape(TOK_DEV, KVH, QPK, HD)
        grad_blk = lax.dynamic_slice_in_dim(grad_output, first_row, TOK_DEV, 0).astype(jnp.float32).reshape(TOK_DEV, KVH, QPK, HD)
        key_blk = lax.dynamic_slice_in_dim(key_padded, first_row, window, 0).astype(jnp.float32).reshape(window, KVH, HD)
        value_blk = lax.dynamic_slice_in_dim(value_padded, first_row, window, 0).astype(jnp.float32).reshape(window, KVH, HD)
        query_pos = first_row + jnp.arange(TOK_DEV, dtype=jnp.int32)
        key_pos = first_row - leading + jnp.arange(window, dtype=jnp.int32)
        row_start = lax.dynamic_slice_in_dim(starts, first_row, TOK_DEV, 0)
        allowed = (key_pos[None, :] >= row_start[:, None]) & (key_pos[None, :] <= query_pos[:, None])
        score = jnp.einsum("tgjd,pgd->gjtp", query_blk, key_blk) * inv_root
        row_top = jnp.max(jnp.where(allowed, score, masked_score), axis=-1)
        row_sum = jnp.sum(jnp.where(allowed, jnp.exp(score - row_top[..., None]), 0.0), axis=-1)
        log_norm = row_top + jnp.log(row_sum)
        weight = jnp.where(allowed, jnp.exp(score - log_norm[..., None]), 0.0)
        weight_b = weight.astype(jnp.bfloat16)
        attended = jnp.einsum("gjtp,pgd->tgjd", weight_b.astype(jnp.float32), value_blk).astype(jnp.bfloat16)
        delta = jnp.sum(grad_blk * attended.astype(jnp.float32), axis=-1).transpose(1, 2, 0)
        dweight = jnp.einsum("tgjd,pgd->gjtp", grad_blk, value_blk)
        dscore = (weight * (dweight - delta[..., None]) * inv_root).astype(jnp.bfloat16)
        grad_query = jnp.einsum("gjtp,pgd->tgjd", dscore.astype(jnp.float32), key_blk).astype(jnp.bfloat16)
        grad_key = jnp.einsum("gjtp,tgjd->pgd", dscore.astype(jnp.float32), query_blk).reshape(window, KVH * HD)
        grad_value = jnp.einsum("gjtp,tgjd->pgd", weight_b.astype(jnp.float32), grad_blk).reshape(window, KVH * HD)
        zero_col = jnp.zeros((), jnp.int32)
        key_old = lax.dynamic_slice(key_acc, (first_row, zero_col), (window, KVH * HD))
        value_old = lax.dynamic_slice(value_acc, (first_row, zero_col), (window, KVH * HD))
        key_acc = lax.dynamic_update_slice(key_acc, key_old + grad_key, (first_row, zero_col))
        value_acc = lax.dynamic_update_slice(value_acc, value_old + grad_value, (first_row, zero_col))
        return (key_acc, value_acc), grad_query.reshape(TOK_DEV, HEADS * HD)

    initial = (jnp.zeros((leading + TOKENS, KVH * HD), jnp.float32), jnp.zeros((leading + TOKENS, KVH * HD), jnp.float32))
    (key_acc, value_acc), grad_rows = lax.scan(one_span, initial, jnp.arange(N_CTX, dtype=jnp.int32))
    grad_query = grad_rows.reshape(TOKENS, HEADS * HD)
    return grad_query, key_acc[leading:].astype(jnp.bfloat16), value_acc[leading:].astype(jnp.bfloat16)
```

```python
import math

import jax
import jax.numpy as jnp
from jax import lax
from jax.experimental import pallas as pl
from jax.experimental.pallas import tpu as pltpu
from jax.sharding import PartitionSpec as P

HEAD = 128
GROUP = 4
BLOCK = 128
OWN = 3
REACH = 9
WINDOW = REACH + OWN - 1
WIDE = GROUP * BLOCK
SPAN = OWN * BLOCK
TAIL = 2 * BLOCK
INV_ROOT = HEAD ** (-0.5)
MIB = 2**20

NT = (((1,), (1,)), ((), ()))
NN = (((1,), (0,)), ((), ()))
VMEM = pl.BlockSpec(memory_space=pltpu.VMEM)
HBM = pl.BlockSpec(memory_space=pltpu.HBM)


def dot(a, b, dims):
    return lax.dot_general(a, b, dims, preferred_element_type=jnp.float32)


def block(index, count=1):
    return slice(index * BLOCK, (index + count) * BLOCK)


def heads_stacked(value):
    return jnp.concatenate([value[:, block(h)] for h in range(GROUP)], axis=0)


def started(pairs, sems):
    copies = [pltpu.make_async_copy(a, b, sems.at[n]) for n, (a, b) in enumerate(pairs)]
    for copy in copies:
        copy.start()
    return copies


def finish(copies):
    for copy in copies:
        copy.wait()


def peer_at(position, parts):
    return lax.rem(position + lax.rem(lax.axis_index("ctx"), 2) * (parts // 2), parts)


def on_odd_core():
    return lax.rem(lax.axis_index("ctx"), 2) == 1


def peer_cols(position, parts):
    return pl.ds(pl.multiple_of(peer_at(position, parts) * WIDE, WIDE), WIDE)


def prepare_kernel(grad_hbm, key_hbm, value_hbm, chunks, pair, tail, sems):
    parts = chunks.shape[0]
    last = slice(SPAN - TAIL, SPAN)
    moves = [
        (key_hbm, pair.at[:, :HEAD]),
        (value_hbm, pair.at[:, HEAD:]),
        (key_hbm.at[last, :], tail.at[:, :HEAD]),
        (value_hbm.at[last, :], tail.at[:, HEAD:]),
    ]
    for p in range(parts):
        moves.append((grad_hbm.at[:, peer_cols(p, parts)], chunks.at[p]))
    finish(started(moves, sems))


def put_window(part, win, own, beside, before, across, apart):
    cols = block(part)
    win[TAIL + 2 * SPAN :, :] = own[:, cols]
    win[TAIL : TAIL + SPAN, :] = before[:, cols]
    odd = on_odd_core()

    @pl.when(odd)
    def _():
        win[TAIL + SPAN : TAIL + 2 * SPAN, :] = beside[:, cols]
        win[0:TAIL, :] = across[SPAN - TAIL :, cols]

    @pl.when(jnp.logical_not(odd))
    def _():
        win[TAIL + SPAN : TAIL + 2 * SPAN, :] = across[:, cols]
        win[0:TAIL, :] = apart[:, cols]


def weight_copy(source, target, sems, i):
    mine = block(i * REACH, REACH)
    return pltpu.make_async_copy(source.at[mine, :], target.at[mine, :], sems.at[i])


def forward_kernel(
    start_hbm, query_hbm, own, beside, before, across, apart,
    weight_hbm, attended_ref, inverse_ref,
    start_ref, query_ref, key_win, value_win, value_t, held, weight_ref, sems, weight_sems
):
    arriving = started([(query_hbm, query_ref), (start_hbm, start_ref)], sems)
    put_window(0, key_win, own, beside, before, across, apart)
    put_window(1, value_win, own, beside, before, across, apart)
    value_t[...] = value_win[...].T
    first = lax.axis_index("ctx") * SPAN - (REACH - 1) * BLOCK
    to_exp2 = INV_ROOT * math.log2(math.e)
    key_at = lax.broadcasted_iota(jnp.int32, (BLOCK, WIDE), 0)
    query_at = lax.broadcasted_iota(jnp.int32, (BLOCK, WIDE), 1) & (BLOCK - 1)
    causal = key_at <= query_at
    finish(arriving)
    for i in range(OWN):
        queries_t = heads_stacked(query_ref[block(i), :]).T
        start = start_ref[i]
        best = jnp.full((8, WIDE), -jnp.inf, jnp.float32)
        for j in range(REACH):
            score = dot(key_win[block(i + j), :], queries_t, NN)
            allowed = causal if j == REACH - 1 else first + (i + j) * BLOCK >= start
            score = jnp.where(allowed, score, -jnp.inf)
            held[block(j), :] = score
            best = jnp.maximum(best, jnp.max(score.reshape(BLOCK // 8, 8, WIDE), axis=0))
        best = jnp.max(best, axis=0, keepdims=True)
        total = jnp.zeros((8, WIDE), jnp.float32)
        for j in range(REACH):
            part = jnp.exp2((held[block(j), :] - best) * to_exp2)
            total = total + jnp.sum(part.reshape(BLOCK // 8, 8, WIDE), axis=0)
            weight_ref[block(i * REACH + j), :] = part.astype(jnp.bfloat16)
        weight_copy(weight_ref, weight_hbm, weight_sems, i).start()
        inverse = 1.0 / jnp.sum(total, axis=0, keepdims=True)
        attended_ref[block(i), :] = (
            dot(value_t[:, block(i, REACH)], weight_ref[block(i * REACH, REACH), :], NN) * inverse
        ).astype(jnp.bfloat16)
        for h in range(GROUP):
            inverse_ref[block(i * GROUP + h), :] = jnp.broadcast_to(
                inverse[:, block(h)], (BLOCK, BLOCK)
            ).T
    for i in range(OWN):
        weight_copy(weight_ref, weight_hbm, weight_sems, i).wait()


def backward_kernel(
    query_hbm, weight_hbm, chunks, own, beside, before, across, apart, attended_ref, inverse_ref,
    dchunks, dnear_far, dmid, dfar, down,
    query_ref, weight_ref, grad_ref, key_win, value_win, key_t, held, dkey, dvalue, dquery,
    sems, weight_sems
):
    parts, share = chunks.shape[0], chunks.shape[1]

    def share_rows(p):
        return pl.ds(pl.multiple_of(peer_at(p, parts) * share, share), share)

    weights_in = [weight_copy(weight_hbm, weight_ref, weight_sems, i) for i in range(OWN)]
    query_in = started([(query_hbm, query_ref)], sems)
    for copy in weights_in:
        copy.start()
    for p in range(parts):
        grad_ref[share_rows(p), :] = chunks[p]
    put_window(1, value_win, own, beside, before, across, apart)
    put_window(0, key_win, own, beside, before, across, apart)
    key_t[...] = key_win[...].T
    finish(query_in)
    on_diagonal = lax.broadcasted_iota(jnp.int32, (BLOCK, BLOCK), 0) == lax.broadcasted_iota(
        jnp.int32, (BLOCK, BLOCK), 1
    )
    for i in range(OWN):
        queries = heads_stacked(query_ref[block(i), :])
        grads = (
            heads_stacked(grad_ref[block(i), :]).astype(jnp.float32)
            * inverse_ref[block(i * GROUP, GROUP), :]
        ).astype(jnp.bfloat16)
        grads_t = grads.T
        deltas = []
        for h in range(GROUP):
            cross = dot(grads[block(h), :], attended_ref[block(i), block(h)], NN)
            deltas.append(jnp.sum(jnp.where(on_diagonal, cross, 0.0), axis=0, keepdims=True))
        delta = jnp.concatenate(deltas, axis=1)
        weights_in[i].wait()
        for j in range(REACH):
            dweight = dot(value_win[block(i + j), :], grads_t, NN)
            weight = weight_ref[block(i * REACH + j), :]
            held[block(i * REACH + j), :] = (
                weight.astype(jnp.float32) * (dweight - delta)
            ).astype(jnp.bfloat16)
        mine = block(i * REACH, REACH)
        turned = dot(key_t[:, block(i, REACH)], held[mine, :], NN) * INV_ROOT
        for h in range(GROUP):
            dquery[block(i), block(h)] = turned[:, block(h)].T.astype(jnp.bfloat16)
        value_part = dot(weight_ref[mine, :], grads, NN)
        key_part = dot(held[mine, :], queries, NN)
        fresh = 0 if i == 0 else REACH - 1
        if fresh:
            seen = slice(0, fresh * BLOCK)
            dvalue[block(i, fresh), :] += value_part[seen, :]
            dkey[block(i, fresh), :] += key_part[seen, :]
        rest = slice(fresh * BLOCK, REACH * BLOCK)
        dvalue[block(i + fresh, REACH - fresh), :] = value_part[rest, :]
        dkey[block(i + fresh, REACH - fresh), :] = key_part[rest, :]
    for p in range(parts):
        dchunks[p] = dquery[share_rows(p), :]

    def put(ref, at, lo, count):
        to, span = slice(at, at + count), slice(lo, lo + count)
        ref[to, :HEAD] = (dkey[span, :] * INV_ROOT).astype(ref.dtype)
        ref[to, HEAD:] = dvalue[span, :].astype(ref.dtype)

    put(dnear_far, 0, TAIL + SPAN, SPAN)
    put(dnear_far, SPAN, 0, TAIL)
    put(dfar, 0, 0, TAIL)
    put(dmid, 0, TAIL, SPAN)
    put(down, 0, TAIL + 2 * SPAN, SPAN)


def merge_kernel(dmid, received, merged):
    odd = on_odd_core()
    f32 = jnp.float32

    @pl.when(odd)
    def _():
        merged[...] = (dmid[...].astype(f32) + received[:SPAN, :].astype(f32)).astype(merged.dtype)

    @pl.when(jnp.logical_not(odd))
    def _():
        head, last = slice(0, SPAN - TAIL), slice(SPAN - TAIL, SPAN)
        merged[head, :] = dmid[head, :]
        merged[last, :] = (
            dmid[last, :].astype(f32) + received[SPAN:, :].astype(f32)
        ).astype(merged.dtype)


def sum_kernel(down, received, shifted, apart, key_hbm, value_hbm, total, out, sems):
    odd = on_odd_core()
    f32 = jnp.float32
    total[...] = down[...] + shifted[...].astype(f32)

    @pl.when(odd)
    def _():
        total[SPAN - TAIL :, :] += apart[...].astype(f32)

    @pl.when(jnp.logical_not(odd))
    def _():
        total[...] += received[:SPAN, :].astype(f32)

    for part in range(2):
        out[part] = total[:, block(part)].astype(out.dtype)
    finish(started([(out.at[0], key_hbm), (out.at[1], value_hbm)], sems))


def place_kernel(chunks, out_hbm, sems):
    parts = chunks.shape[0]
    finish(
        started([(chunks.at[p], out_hbm.at[:, peer_cols(p, parts)]) for p in range(parts)], sems)
    )


def passed_along(value, by, parities=(0, 1)):
    length = lax.axis_size("ctx")
    pairs = [
        (i, i + by) for i in range(length) if 0 <= i + by < length and i % 2 in parities
    ]
    return lax.ppermute(value, "ctx", pairs)


def core_swapped(value):
    return lax.ppermute(value, "ctx", [(i, i ^ 1) for i in range(lax.axis_size("ctx"))])


def pinned(*arrays):
    return [pltpu.with_memory_space_constraint(x, pltpu.HBM) for x in arrays]


def cost(flops, exps=0):
    return pl.CostEstimate(flops=int(flops), bytes_accessed=8 * MIB, transcendentals=int(exps))


def params(mib):
    return pltpu.CompilerParams(vmem_limit_bytes=mib * MIB)


def body(query_states, key_states, value_states, grad_output, doc_start):
    parts, length = lax.axis_size("kvh"), lax.axis_size("ctx")
    share = SPAN // parts
    bf16, f32 = jnp.bfloat16, jnp.float32
    sds = jax.ShapeDtypeStruct
    dma = pltpu.SemaphoreType.DMA
    window = WINDOW * BLOCK
    pairs = OWN * REACH
    flops = 2 * pairs * BLOCK * BLOCK * WIDE
    chunked = sds((parts, share, WIDE), bf16)
    pair = sds((SPAN, 2 * HEAD), bf16)
    tail = sds((TAIL, 2 * HEAD), bf16)
    rings = [
        [c * parts + (p + (c % 2) * (parts // 2)) % parts for p in range(parts)]
        for c in range(length)
    ]

    def exchanged(value):
        return lax.all_to_all(
            value, ("ctx", "kvh"), split_axis=0, concat_axis=0, axis_index_groups=rings, tiled=True
        )

    start_hbm, query_hbm = pinned(doc_start, query_states)
    chunks, own, last = pl.pallas_call(
        prepare_kernel,
        out_shape=(chunked, pair, tail),
        in_specs=[HBM] * 3,
        out_specs=(VMEM,) * 3,
        scratch_shapes=[dma((parts + 4,))],
        compiler_params=params(4),
        name="prepare",
    )(*pinned(grad_output, key_states, value_states))
    grads = exchanged(chunks)
    before = passed_along(own, 2)
    apart = passed_along(last, 3, (1,))
    beside = passed_along(own, 1, (0,))
    across = core_swapped(before)
    halo = (own, beside, before, across, apart)

    weight, attended, inverse = pl.pallas_call(
        forward_kernel,
        out_shape=(
            sds((pairs * BLOCK, WIDE), bf16),
            sds((OWN * HEAD, WIDE), bf16),
            sds((OWN * WIDE, HEAD), f32),
        ),
        in_specs=[HBM, HBM] + [VMEM] * 5,
        out_specs=(HBM, VMEM, VMEM),
        scratch_shapes=[
            pltpu.SMEM(doc_start.shape, jnp.int32),
            pltpu.VMEM((SPAN, WIDE), bf16),
            pltpu.VMEM((window, HEAD), bf16),
            pltpu.VMEM((window, HEAD), bf16),
            pltpu.VMEM((HEAD, window), bf16),
            pltpu.VMEM((REACH * BLOCK, WIDE), f32),
            pltpu.VMEM((pairs * BLOCK, WIDE), bf16),
            dma((2,)),
            dma((OWN,)),
        ],
        cost_estimate=cost(2 * flops, pairs * BLOCK * WIDE),
        compiler_params=params(16),
        name="forward",
    )(start_hbm, query_hbm, *halo)

    dchunks, dnear_far, dmid, dfar, down = pl.pallas_call(
        backward_kernel,
        out_shape=(
            chunked,
            sds((SPAN + TAIL, 2 * HEAD), bf16),
            pair,
            tail,
            sds((SPAN, 2 * HEAD), f32),
        ),
        in_specs=[HBM, HBM] + [VMEM] * 8,
        out_specs=(VMEM,) * 5,
        scratch_shapes=[
            pltpu.VMEM((SPAN, WIDE), bf16),
            pltpu.VMEM((pairs * BLOCK, WIDE), bf16),
            pltpu.VMEM((SPAN, WIDE), bf16),
            pltpu.VMEM((window, HEAD), bf16),
            pltpu.VMEM((window, HEAD), bf16),
            pltpu.VMEM((HEAD, window), bf16),
            pltpu.VMEM((pairs * BLOCK, WIDE), bf16),
            pltpu.VMEM((window, HEAD), f32),
            pltpu.VMEM((window, HEAD), f32),
            pltpu.VMEM((SPAN, WIDE), bf16),
            dma((1,)),
            dma((OWN,)),
        ],
        cost_estimate=cost(4 * flops),
        compiler_params=params(24),
        name="backward",
    )(query_hbm, *pinned(weight), grads, *halo, attended, inverse)

    back = exchanged(dchunks)
    received = core_swapped(dnear_far)
    far_back = passed_along(dfar, -3, (0,))
    merged = pl.pallas_call(
        merge_kernel,
        out_shape=pair,
        in_specs=[VMEM] * 2,
        out_specs=VMEM,
        compiler_params=params(4),
        name="merge",
    )(dmid, received)
    shifted = passed_along(merged, -2)
    grad_key, grad_value = pl.pallas_call(
        sum_kernel,
        out_shape=(sds((SPAN, HEAD), bf16),) * 2,
        in_specs=[VMEM] * 4,
        out_specs=(HBM,) * 2,
        scratch_shapes=[
            pltpu.VMEM((SPAN, 2 * HEAD), f32), pltpu.VMEM((2, SPAN, HEAD), bf16), dma((2,))
        ],
        compiler_params=params(4),
        name="sum",
    )(down, received, shifted, far_back)
    grad_query = pl.pallas_call(
        place_kernel,
        out_shape=sds((share, parts * WIDE), bf16),
        in_specs=[VMEM],
        out_specs=HBM,
        scratch_shapes=[dma((parts,))],
        compiler_params=params(4),
        name="place",
    )(back)
    return grad_query, grad_key, grad_value


def solution(mesh):
    in_specs = (
        P("ctx", "kvh"),
        P("ctx", "kvh"),
        P("ctx", "kvh"),
        P(("ctx", "kvh"), None),
        P("ctx"),
    )
    out_specs = (P(("ctx", "kvh"), None), P("ctx", "kvh"), P("ctx", "kvh"))
    return jax.shard_map(body, mesh=mesh, in_specs=in_specs, out_specs=out_specs, check_vma=False)
```

```python
import math

import jax
import jax.numpy as jnp
from jax import lax
from jax.experimental import pallas as pl
from jax.experimental.pallas import tpu as pltpu
from jax.sharding import PartitionSpec as P

HEAD = 128
GROUP = 4
BLOCK = 128
OWN = 3
REACH = 9
WINDOW = REACH + OWN - 1
WIDE = GROUP * BLOCK
SPAN = OWN * BLOCK
TAIL = 2 * BLOCK
INV_ROOT = HEAD ** (-0.5)
MIB = 2**20

NT = (((1,), (1,)), ((), ()))
NN = (((1,), (0,)), ((), ()))
VMEM = pl.BlockSpec(memory_space=pltpu.VMEM)
HBM = pl.BlockSpec(memory_space=pltpu.HBM)


def dot(a, b, dims):
    return lax.dot_general(a, b, dims, preferred_element_type=jnp.float32)


def block(index, count=1):
    return slice(index * BLOCK, (index + count) * BLOCK)


def heads_stacked(value):
    return jnp.concatenate([value[:, block(h)] for h in range(GROUP)], axis=0)


def started(pairs, sems):
    copies = [pltpu.make_async_copy(a, b, sems.at[n]) for n, (a, b) in enumerate(pairs)]
    for copy in copies:
        copy.start()
    return copies


def finish(copies):
    for copy in copies:
        copy.wait()


def peer_at(position, parts):
    return lax.rem(position + lax.rem(lax.axis_index("ctx"), 2) * (parts // 2), parts)


def on_odd_core():
    return lax.rem(lax.axis_index("ctx"), 2) == 1


def peer_cols(position, parts):
    return pl.ds(pl.multiple_of(peer_at(position, parts) * WIDE, WIDE), WIDE)


def pair_kernel(key_hbm, value_hbm, pair, tail, sems):
    last = slice(SPAN - TAIL, SPAN)
    moves = [
        (key_hbm, pair.at[:, :HEAD]),
        (value_hbm, pair.at[:, HEAD:]),
        (key_hbm.at[last, :], tail.at[:, :HEAD]),
        (value_hbm.at[last, :], tail.at[:, HEAD:]),
    ]
    finish(started(moves, sems))


def chunk_kernel(grad_hbm, before, apart, chunks, sems):
    parts = chunks.shape[0]
    finish(
        started([(grad_hbm.at[:, peer_cols(p, parts)], chunks.at[p]) for p in range(parts)], sems)
    )


def put_window(part, win, own, beside, before, across, apart):
    cols = block(part)
    win[TAIL + 2 * SPAN :, :] = own[:, cols]
    win[TAIL : TAIL + SPAN, :] = before[:, cols]
    odd = on_odd_core()

    @pl.when(odd)
    def _():
        win[TAIL + SPAN : TAIL + 2 * SPAN, :] = beside[:, cols]
        win[0:TAIL, :] = across[SPAN - TAIL :, cols]

    @pl.when(jnp.logical_not(odd))
    def _():
        win[TAIL + SPAN : TAIL + 2 * SPAN, :] = across[:, cols]
        win[0:TAIL, :] = apart[:, cols]


def weight_copy(source, target, sems, i):
    mine = block(i * REACH, REACH)
    return pltpu.make_async_copy(source.at[mine, :], target.at[mine, :], sems.at[i])


def forward_kernel(
    start_hbm, query_hbm, own, beside, before, across, apart,
    weight_hbm, attended_ref, inverse_ref, value_win, key_t,
    start_ref, query_ref, key_win, value_t, held, weight_ref, sems, weight_sems
):
    arriving = started([(query_hbm, query_ref), (start_hbm, start_ref)], sems)
    put_window(0, key_win, own, beside, before, across, apart)
    put_window(1, value_win, own, beside, before, across, apart)
    value_t[...] = value_win[...].T
    key_t[...] = key_win[...].T
    first = lax.axis_index("ctx") * SPAN - (REACH - 1) * BLOCK
    to_exp2 = INV_ROOT * math.log2(math.e)
    key_at = lax.broadcasted_iota(jnp.int32, (BLOCK, WIDE), 0)
    query_at = lax.broadcasted_iota(jnp.int32, (BLOCK, WIDE), 1) & (BLOCK - 1)
    causal = key_at <= query_at
    finish(arriving)
    for i in range(OWN):
        queries_t = heads_stacked(query_ref[block(i), :]).T
        start = start_ref[i]
        best = jnp.full((8, WIDE), -jnp.inf, jnp.float32)
        for j in range(REACH):
            score = dot(key_win[block(i + j), :], queries_t, NN)
            allowed = causal if j == REACH - 1 else first + (i + j) * BLOCK >= start
            score = jnp.where(allowed, score, -jnp.inf)
            held[block(j), :] = score
            best = jnp.maximum(best, jnp.max(score.reshape(BLOCK // 8, 8, WIDE), axis=0))
        best = jnp.max(best, axis=0, keepdims=True)
        total = jnp.zeros((8, WIDE), jnp.float32)
        for j in range(REACH):
            part = jnp.exp2((held[block(j), :] - best) * to_exp2)
            total = total + jnp.sum(part.reshape(BLOCK // 8, 8, WIDE), axis=0)
            weight_ref[block(i * REACH + j), :] = part.astype(jnp.bfloat16)
        weight_copy(weight_ref, weight_hbm, weight_sems, i).start()
        inverse = 1.0 / jnp.sum(total, axis=0, keepdims=True)
        attended_ref[block(i), :] = (
            dot(value_t[:, block(i, REACH)], weight_ref[block(i * REACH, REACH), :], NN) * inverse
        ).astype(jnp.bfloat16)
        for h in range(GROUP):
            inverse_ref[block(i * GROUP + h), :] = jnp.broadcast_to(
                inverse[:, block(h)], (BLOCK, BLOCK)
            ).T
    for i in range(OWN):
        weight_copy(weight_ref, weight_hbm, weight_sems, i).wait()


def backward_kernel(
    query_hbm, weight_hbm, chunks, value_win, key_t, attended_ref, inverse_ref,
    dchunks, dnear_far, dmid, dfar, down,
    query_ref, weight_ref, grad_ref, wide, held, dkey, dvalue, dquery, sems, weight_sems
):
    parts, share = chunks.shape[0], chunks.shape[1]

    def share_rows(p):
        return pl.ds(pl.multiple_of(peer_at(p, parts) * share, share), share)

    weights_in = [weight_copy(weight_hbm, weight_ref, weight_sems, i) for i in range(OWN)]
    for copy in weights_in:
        copy.start()
    query_in = started([(query_hbm, query_ref)], sems)
    for p in range(parts):
        grad_ref[share_rows(p), :] = chunks[p]
    on_diagonal = lax.broadcasted_iota(jnp.int32, (BLOCK, BLOCK), 0) == lax.broadcasted_iota(
        jnp.int32, (BLOCK, BLOCK), 1
    )
    for i in range(OWN):
        grads = (
            heads_stacked(grad_ref[block(i), :]).astype(jnp.float32)
            * inverse_ref[block(i * GROUP, GROUP), :]
        ).astype(jnp.bfloat16)
        grads_t = grads.T
        deltas = []
        for h in range(GROUP):
            cross = dot(grads[block(h), :], attended_ref[block(i), block(h)], NN)
            deltas.append(jnp.sum(jnp.where(on_diagonal, cross, 0.0), axis=0, keepdims=True))
        delta = jnp.concatenate(deltas, axis=1)

        def slope(j):
            return dot(value_win[block(i + j), :], grads_t, NN) - delta

        if i == 0:
            for j in range(REACH):
                wide[block(j), :] = slope(j)
            finish(query_in)
        weights_in[i].wait()
        for j in range(REACH):
            weight = weight_ref[block(i * REACH + j), :].astype(jnp.float32)
            held[block(i * REACH + j), :] = (
                weight * (wide[block(j), :] if i == 0 else slope(j))
            ).astype(jnp.bfloat16)
        queries = heads_stacked(query_ref[block(i), :])
        mine = block(i * REACH, REACH)
        turned = dot(key_t[:, block(i, REACH)], held[mine, :], NN) * INV_ROOT
        for h in range(GROUP):
            dquery[block(i), block(h)] = turned[:, block(h)].T.astype(jnp.bfloat16)
        value_part = dot(weight_ref[mine, :], grads, NN)
        key_part = dot(held[mine, :], queries, NN)
        fresh = 0 if i == 0 else REACH - 1
        if fresh:
            seen = slice(0, fresh * BLOCK)
            dvalue[block(i, fresh), :] += value_part[seen, :]
            dkey[block(i, fresh), :] += key_part[seen, :]
        rest = slice(fresh * BLOCK, REACH * BLOCK)
        dvalue[block(i + fresh, REACH - fresh), :] = value_part[rest, :]
        dkey[block(i + fresh, REACH - fresh), :] = key_part[rest, :]
    for p in range(parts):
        dchunks[p] = dquery[share_rows(p), :]

    def put(ref, at, lo, count):
        to, span = slice(at, at + count), slice(lo, lo + count)
        ref[to, :HEAD] = (dkey[span, :] * INV_ROOT).astype(ref.dtype)
        ref[to, HEAD:] = dvalue[span, :].astype(ref.dtype)

    put(dnear_far, 0, TAIL + SPAN, SPAN)
    put(dnear_far, SPAN, 0, TAIL)
    put(dfar, 0, 0, TAIL)
    put(dmid, 0, TAIL, SPAN)
    put(down, 0, TAIL + 2 * SPAN, SPAN)


def merge_kernel(dmid, received, merged):
    odd = on_odd_core()
    f32 = jnp.float32

    @pl.when(odd)
    def _():
        merged[...] = (dmid[...].astype(f32) + received[:SPAN, :].astype(f32)).astype(merged.dtype)

    @pl.when(jnp.logical_not(odd))
    def _():
        head, last = slice(0, SPAN - TAIL), slice(SPAN - TAIL, SPAN)
        merged[head, :] = dmid[head, :]
        merged[last, :] = (
            dmid[last, :].astype(f32) + received[SPAN:, :].astype(f32)
        ).astype(merged.dtype)


def fold_kernel(down, received, apart, folded):
    odd = on_odd_core()
    f32 = jnp.float32

    @pl.when(odd)
    def _():
        head, last = slice(0, SPAN - TAIL), slice(SPAN - TAIL, SPAN)
        folded[head, :] = down[head, :]
        folded[last, :] = down[last, :] + apart[...].astype(f32)

    @pl.when(jnp.logical_not(odd))
    def _():
        folded[...] = down[...] + received[:SPAN, :].astype(f32)


def sum_kernel(folded, shifted, key_hbm, value_hbm, out, sems):
    total = folded[...] + shifted[...].astype(jnp.float32)
    for part in range(2):
        out[part] = total[:, block(part)].astype(out.dtype)
    finish(started([(out.at[0], key_hbm), (out.at[1], value_hbm)], sems))


def place_kernel(chunks, out_hbm, sems):
    parts = chunks.shape[0]
    finish(
        started([(chunks.at[p], out_hbm.at[:, peer_cols(p, parts)]) for p in range(parts)], sems)
    )


def passed_along(value, by, parities=(0, 1)):
    length = lax.axis_size("ctx")
    pairs = [
        (i, i + by) for i in range(length) if 0 <= i + by < length and i % 2 in parities
    ]
    return lax.ppermute(value, "ctx", pairs)


def core_swapped(value):
    return lax.ppermute(value, "ctx", [(i, i ^ 1) for i in range(lax.axis_size("ctx"))])


def pinned(*arrays):
    return [pltpu.with_memory_space_constraint(x, pltpu.HBM) for x in arrays]


def cost(flops, exps=0):
    return pl.CostEstimate(flops=int(flops), bytes_accessed=8 * MIB, transcendentals=int(exps))


def params(mib):
    return pltpu.CompilerParams(vmem_limit_bytes=mib * MIB)


def body(query_states, key_states, value_states, grad_output, doc_start):
    parts, length = lax.axis_size("kvh"), lax.axis_size("ctx")
    share = SPAN // parts
    bf16, f32 = jnp.bfloat16, jnp.float32
    sds = jax.ShapeDtypeStruct
    dma = pltpu.SemaphoreType.DMA
    window = WINDOW * BLOCK
    pairs = OWN * REACH
    flops = 2 * pairs * BLOCK * BLOCK * WIDE
    chunked = sds((parts, share, WIDE), bf16)
    pair = sds((SPAN, 2 * HEAD), bf16)
    tail = sds((TAIL, 2 * HEAD), bf16)
    rings = [
        [c * parts + (p + (c % 2) * (parts // 2)) % parts for p in range(parts)]
        for c in range(length)
    ]

    def exchanged(value):
        return lax.all_to_all(
            value, ("ctx", "kvh"), split_axis=0, concat_axis=0, axis_index_groups=rings, tiled=True
        )

    start_hbm, query_hbm = pinned(doc_start, query_states)
    own, last = pl.pallas_call(
        pair_kernel,
        out_shape=(pair, tail),
        in_specs=[HBM] * 2,
        out_specs=(VMEM,) * 2,
        scratch_shapes=[dma((4,))],
        compiler_params=params(4),
        name="pair",
    )(*pinned(key_states, value_states))
    before = passed_along(own, 2)
    apart = passed_along(last, 3, (1,))
    beside = passed_along(own, 1, (0,))
    across = core_swapped(before)
    halo = (own, beside, before, across, apart)
    chunks = pl.pallas_call(
        chunk_kernel,
        out_shape=chunked,
        in_specs=[HBM, VMEM, VMEM],
        out_specs=VMEM,
        scratch_shapes=[dma((parts,))],
        compiler_params=params(4),
        name="chunk",
    )(*pinned(grad_output), before, apart)
    grads = exchanged(chunks)

    weight, attended, inverse, value_win, key_t = pl.pallas_call(
        forward_kernel,
        out_shape=(
            sds((pairs * BLOCK, WIDE), bf16),
            sds((OWN * HEAD, WIDE), bf16),
            sds((OWN * WIDE, HEAD), f32),
            sds((window, HEAD), bf16),
            sds((HEAD, window), bf16),
        ),
        in_specs=[HBM, HBM] + [VMEM] * 5,
        out_specs=(HBM,) + (VMEM,) * 4,
        scratch_shapes=[
            pltpu.SMEM(doc_start.shape, jnp.int32),
            pltpu.VMEM((SPAN, WIDE), bf16),
            pltpu.VMEM((window, HEAD), bf16),
            pltpu.VMEM((HEAD, window), bf16),
            pltpu.VMEM((REACH * BLOCK, WIDE), f32),
            pltpu.VMEM((pairs * BLOCK, WIDE), bf16),
            dma((2,)),
            dma((OWN,)),
        ],
        cost_estimate=cost(2 * flops, pairs * BLOCK * WIDE),
        compiler_params=params(16),
        name="forward",
    )(start_hbm, query_hbm, *halo)

    dchunks, dnear_far, dmid, dfar, down = pl.pallas_call(
        backward_kernel,
        out_shape=(
            chunked,
            sds((SPAN + TAIL, 2 * HEAD), bf16),
            pair,
            tail,
            sds((SPAN, 2 * HEAD), f32),
        ),
        in_specs=[HBM, HBM] + [VMEM] * 5,
        out_specs=(VMEM,) * 5,
        scratch_shapes=[
            pltpu.VMEM((SPAN, WIDE), bf16),
            pltpu.VMEM((pairs * BLOCK, WIDE), bf16),
            pltpu.VMEM((SPAN, WIDE), bf16),
            pltpu.VMEM((REACH * BLOCK, WIDE), f32),
            pltpu.VMEM((pairs * BLOCK, WIDE), bf16),
            pltpu.VMEM((window, HEAD), f32),
            pltpu.VMEM((window, HEAD), f32),
            pltpu.VMEM((SPAN, WIDE), bf16),
            dma((1,)),
            dma((OWN,)),
        ],
        cost_estimate=cost(4 * flops),
        compiler_params=params(24),
        name="backward",
    )(query_hbm, *pinned(weight), grads, value_win, key_t, attended, inverse)

    back = exchanged(dchunks)
    received = core_swapped(dnear_far)
    far_back = passed_along(dfar, -3, (0,))
    merged = pl.pallas_call(
        merge_kernel,
        out_shape=pair,
        in_specs=[VMEM] * 2,
        out_specs=VMEM,
        compiler_params=params(4),
        name="merge",
    )(dmid, received)
    shifted = passed_along(merged, -2)
    folded = pl.pallas_call(
        fold_kernel,
        out_shape=sds((SPAN, 2 * HEAD), f32),
        in_specs=[VMEM] * 3,
        out_specs=VMEM,
        compiler_params=params(4),
        name="fold",
    )(down, received, far_back)
    grad_key, grad_value = pl.pallas_call(
        sum_kernel,
        out_shape=(sds((SPAN, HEAD), bf16),) * 2,
        in_specs=[VMEM] * 2,
        out_specs=(HBM,) * 2,
        scratch_shapes=[pltpu.VMEM((2, SPAN, HEAD), bf16), dma((2,))],
        compiler_params=params(4),
        name="sum",
    )(folded, shifted)
    grad_query = pl.pallas_call(
        place_kernel,
        out_shape=sds((share, parts * WIDE), bf16),
        in_specs=[VMEM],
        out_specs=HBM,
        scratch_shapes=[dma((parts,))],
        compiler_params=params(4),
        name="place",
    )(back)
    return grad_query, grad_key, grad_value


def solution(mesh):
    in_specs = (
        P("ctx", "kvh"),
        P("ctx", "kvh"),
        P("ctx", "kvh"),
        P(("ctx", "kvh"), None),
        P("ctx"),
    )
    out_specs = (P(("ctx", "kvh"), None), P("ctx", "kvh"), P("ctx", "kvh"))
    return jax.shard_map(body, mesh=mesh, in_specs=in_specs, out_specs=out_specs, check_vma=False)
```

```python
import math

import jax
import jax.numpy as jnp
from jax import lax
from jax.experimental import pallas as pl
from jax.experimental.pallas import tpu as pltpu
from jax.sharding import PartitionSpec as P

HEAD = 128
GROUP = 4
BLOCK = 128
OWN = 3
REACH = 9
WINDOW = REACH + OWN - 1
WIDE = GROUP * BLOCK
SPAN = OWN * BLOCK
TAIL = 2 * BLOCK
INV_ROOT = HEAD ** (-0.5)
TO_EXP2 = INV_ROOT * math.log2(math.e)
MIB = 2**20

NT = (((1,), (1,)), ((), ()))
NN = (((1,), (0,)), ((), ()))
VMEM = pl.BlockSpec(memory_space=pltpu.VMEM)
HBM = pl.BlockSpec(memory_space=pltpu.HBM)


def dot(a, b, dims):
    return lax.dot_general(a, b, dims, preferred_element_type=jnp.float32)


def block(index, count=1):
    return slice(index * BLOCK, (index + count) * BLOCK)


def heads_stacked(value):
    return jnp.concatenate([value[:, block(h)] for h in range(GROUP)], axis=0)


def started(pairs, sems):
    copies = [pltpu.make_async_copy(a, b, sems.at[n]) for n, (a, b) in enumerate(pairs)]
    for copy in copies:
        copy.start()
    return copies


def finish(copies):
    for copy in copies:
        copy.wait()


def peer_at(position, parts):
    return lax.rem(position + lax.rem(lax.axis_index("ctx"), 2) * (parts // 2), parts)


def on_odd_core():
    return lax.rem(lax.axis_index("ctx"), 2) == 1


def peer_cols(position, parts):
    return pl.ds(pl.multiple_of(peer_at(position, parts) * WIDE, WIDE), WIDE)


def prepare_kernel(grad_hbm, key_hbm, value_hbm, chunks, pair, tail, sems):
    parts = chunks.shape[0]
    last = slice(SPAN - TAIL, SPAN)
    moves = [(grad_hbm.at[:, peer_cols(p, parts)], chunks.at[p]) for p in range(parts)]
    moves += [
        (key_hbm, pair.at[:, :HEAD]),
        (value_hbm, pair.at[:, HEAD:]),
        (key_hbm.at[last, :], tail.at[:, :HEAD]),
        (value_hbm.at[last, :], tail.at[:, HEAD:]),
    ]
    finish(started(moves, sems))


def halo_kernel(own, beside, apart, keys, values):
    odd = on_odd_core()
    for part, win in enumerate((keys, values)):
        cols = block(part)
        win[TAIL + 2 * SPAN :, :] = own[:, cols]

        @pl.when(odd)
        def _():
            win[0:TAIL, :] = jnp.zeros((TAIL, HEAD), win.dtype)
            win[TAIL + SPAN : TAIL + 2 * SPAN, :] = beside[:, cols]

        @pl.when(jnp.logical_not(odd))
        def _():
            win[0:TAIL, :] = apart[:, cols]
            win[TAIL + SPAN : TAIL + 2 * SPAN, :] = jnp.zeros((SPAN, HEAD), win.dtype)

        win[TAIL : TAIL + SPAN, :] = jnp.zeros((SPAN, HEAD), win.dtype)


def complete(win, part, partial, before, across):
    cols = block(part)
    win[...] = partial[...]
    win[TAIL : TAIL + SPAN, :] = before[:, cols]
    odd = on_odd_core()

    @pl.when(odd)
    def _():
        win[0:TAIL, :] = across[SPAN - TAIL :, cols]

    @pl.when(jnp.logical_not(odd))
    def _():
        win[TAIL + SPAN : TAIL + 2 * SPAN, :] = across[:, cols]


def causal_mask():
    key_at = lax.broadcasted_iota(jnp.int32, (BLOCK, WIDE), 0)
    query_at = lax.broadcasted_iota(jnp.int32, (BLOCK, WIDE), 1) & (BLOCK - 1)
    return key_at <= query_at


def first_key():
    return lax.axis_index("ctx") * SPAN - (REACH - 1) * BLOCK


def row8(i):
    return slice(8 * i, 8 * i + 8)


def forward_kernel(
    start_hbm, query_hbm, keys, values, before, across,
    queries, queries_t, key_win, value_win, key_t, attended_ref, norm_ref, starts,
    start_ref, query_ref, value_t, held, weights, sems
):
    arriving = started([(query_hbm, query_ref), (start_hbm, start_ref)], sems)
    complete(key_win, 0, keys, before, across)
    complete(value_win, 1, values, before, across)
    value_t[...] = value_win[...].T
    key_t[...] = key_win[...].T
    causal = causal_mask()
    first = first_key()
    finish(arriving)
    for i in range(OWN):
        stacked = heads_stacked(query_ref[block(i), :])
        queries[block(i * GROUP, GROUP), :] = stacked
        turned = stacked.T
        queries_t[block(i), :] = turned
        start = start_ref[i]
        starts[row8(i), :] = jnp.full((8, WIDE), start, jnp.int32)
        best = jnp.full((8, WIDE), -jnp.inf, jnp.float32)
        for j in range(REACH):
            score = dot(key_win[block(i + j), :], turned, NN)
            allowed = causal if j == REACH - 1 else first + (i + j) * BLOCK >= start
            score = jnp.where(allowed, score, -jnp.inf)
            held[block(j), :] = score
            best = jnp.maximum(best, jnp.max(score.reshape(BLOCK // 8, 8, WIDE), axis=0))
        best = jnp.max(best, axis=0, keepdims=True)
        total = jnp.zeros((8, WIDE), jnp.float32)
        for j in range(REACH):
            part = jnp.exp2((held[block(j), :] - best) * TO_EXP2)
            total = total + jnp.sum(part.reshape(BLOCK // 8, 8, WIDE), axis=0)
            weights[block(i * REACH + j), :] = part.astype(jnp.bfloat16)
        total = jnp.sum(total, axis=0, keepdims=True)
        norm_ref[row8(i), :] = jnp.broadcast_to(best * TO_EXP2 + jnp.log2(total), (8, WIDE))
        attended_ref[block(i), :] = (
            dot(value_t[:, block(i, REACH)], weights[block(i * REACH, REACH), :], NN)
            * (1.0 / total)
        ).astype(jnp.bfloat16)


def backward_kernel(
    chunks, queries, queries_t, key_win, value_win, key_t, attended_ref, norm_ref, starts,
    dchunks, dnear_far, dmid, dfar, down,
    grad_ref, weights, held, dkey, dvalue, dquery
):
    parts, share = chunks.shape[0], chunks.shape[1]

    def share_rows(p):
        return pl.ds(pl.multiple_of(peer_at(p, parts) * share, share), share)

    for p in range(parts):
        grad_ref[share_rows(p), :] = chunks[p]
    causal = causal_mask()
    first = first_key()
    on_diagonal = lax.broadcasted_iota(jnp.int32, (BLOCK, BLOCK), 0) == lax.broadcasted_iota(
        jnp.int32, (BLOCK, BLOCK), 1
    )
    for i in range(OWN):
        grads = heads_stacked(grad_ref[block(i), :])
        grads_t = grads.T
        deltas = []
        for h in range(GROUP):
            cross = dot(grads[block(h), :], attended_ref[block(i), block(h)], NN)
            deltas.append(jnp.sum(jnp.where(on_diagonal, cross, 0.0), axis=0, keepdims=True))
        delta = jnp.concatenate(deltas, axis=1)
        norm = norm_ref[8 * i : 8 * i + 1, :]
        start = starts[8 * i : 8 * i + 1, :]
        for j in range(REACH):
            score = dot(key_win[block(i + j), :], queries_t[block(i), :], NN)
            if j == REACH - 1:
                weight = jnp.where(causal, jnp.exp2(score * TO_EXP2 - norm), 0.0)
            else:
                allowed = first + (i + j) * BLOCK >= start
                weight = jnp.exp2(score * TO_EXP2 - jnp.where(allowed, norm, jnp.inf))
            dweight = dot(value_win[block(i + j), :], grads_t, NN)
            weights[block(i * REACH + j), :] = weight.astype(jnp.bfloat16)
            held[block(i * REACH + j), :] = (weight * (dweight - delta)).astype(jnp.bfloat16)
        mine = block(i * REACH, REACH)
        turned = dot(key_t[:, block(i, REACH)], held[mine, :], NN) * INV_ROOT
        for h in range(GROUP):
            dquery[block(i), block(h)] = turned[:, block(h)].T.astype(jnp.bfloat16)
        value_part = dot(weights[mine, :], grads, NN)
        key_part = dot(held[mine, :], queries[block(i * GROUP, GROUP), :], NN)
        fresh = 0 if i == 0 else REACH - 1
        if fresh:
            seen = slice(0, fresh * BLOCK)
            dvalue[block(i, fresh), :] += value_part[seen, :]
            dkey[block(i, fresh), :] += key_part[seen, :]
        rest = slice(fresh * BLOCK, REACH * BLOCK)
        dvalue[block(i + fresh, REACH - fresh), :] = value_part[rest, :]
        dkey[block(i + fresh, REACH - fresh), :] = key_part[rest, :]
    for p in range(parts):
        dchunks[p] = dquery[share_rows(p), :]

    def put(ref, at, lo, count):
        to, span = slice(at, at + count), slice(lo, lo + count)
        ref[to, :HEAD] = (dkey[span, :] * INV_ROOT).astype(ref.dtype)
        ref[to, HEAD:] = dvalue[span, :].astype(ref.dtype)

    put(dnear_far, 0, TAIL + SPAN, SPAN)
    put(dnear_far, SPAN, 0, TAIL)
    put(dfar, 0, 0, TAIL)
    put(dmid, 0, TAIL, SPAN)
    put(down, 0, TAIL + 2 * SPAN, SPAN)


def merge_kernel(dmid, received, merged):
    odd = on_odd_core()
    f32 = jnp.float32

    @pl.when(odd)
    def _():
        merged[...] = (dmid[...].astype(f32) + received[:SPAN, :].astype(f32)).astype(merged.dtype)

    @pl.when(jnp.logical_not(odd))
    def _():
        head, last = slice(0, SPAN - TAIL), slice(SPAN - TAIL, SPAN)
        merged[head, :] = dmid[head, :]
        merged[last, :] = (
            dmid[last, :].astype(f32) + received[SPAN:, :].astype(f32)
        ).astype(merged.dtype)


def fold_kernel(down, received, apart, folded):
    odd = on_odd_core()
    f32 = jnp.float32

    @pl.when(odd)
    def _():
        head, last = slice(0, SPAN - TAIL), slice(SPAN - TAIL, SPAN)
        folded[head, :] = down[head, :]
        folded[last, :] = down[last, :] + apart[...].astype(f32)

    @pl.when(jnp.logical_not(odd))
    def _():
        folded[...] = down[...] + received[:SPAN, :].astype(f32)


def sum_kernel(folded, shifted, key_hbm, value_hbm, out, sems):
    total = folded[...] + shifted[...].astype(jnp.float32)
    for part in range(2):
        out[part] = total[:, block(part)].astype(out.dtype)
    finish(started([(out.at[0], key_hbm), (out.at[1], value_hbm)], sems))


def place_kernel(chunks, out_hbm, sems):
    parts = chunks.shape[0]
    finish(
        started([(chunks.at[p], out_hbm.at[:, peer_cols(p, parts)]) for p in range(parts)], sems)
    )


def passed_along(value, by, parities=(0, 1)):
    length = lax.axis_size("ctx")
    pairs = [
        (i, i + by) for i in range(length) if 0 <= i + by < length and i % 2 in parities
    ]
    return lax.ppermute(value, "ctx", pairs)


def core_swapped(value):
    return lax.ppermute(value, "ctx", [(i, i ^ 1) for i in range(lax.axis_size("ctx"))])


def pinned(*arrays):
    return [pltpu.with_memory_space_constraint(x, pltpu.HBM) for x in arrays]


def cost(flops, exps=0):
    return pl.CostEstimate(flops=int(flops), bytes_accessed=8 * MIB, transcendentals=int(exps))


def params(mib):
    return pltpu.CompilerParams(vmem_limit_bytes=mib * MIB)


def body(query_states, key_states, value_states, grad_output, doc_start):
    parts, length = lax.axis_size("kvh"), lax.axis_size("ctx")
    share = SPAN // parts
    bf16, f32 = jnp.bfloat16, jnp.float32
    sds = jax.ShapeDtypeStruct
    dma = pltpu.SemaphoreType.DMA
    window = WINDOW * BLOCK
    pairs = OWN * REACH
    flops = 2 * pairs * BLOCK * BLOCK * WIDE
    chunked = sds((parts, share, WIDE), bf16)
    pair = sds((SPAN, 2 * HEAD), bf16)
    tail = sds((TAIL, 2 * HEAD), bf16)
    rings = [
        [c * parts + (p + (c % 2) * (parts // 2)) % parts for p in range(parts)]
        for c in range(length)
    ]

    def exchanged(value):
        return lax.all_to_all(
            value, ("ctx", "kvh"), split_axis=0, concat_axis=0, axis_index_groups=rings, tiled=True
        )

    start_hbm, query_hbm = pinned(doc_start, query_states)
    chunks, own, last = pl.pallas_call(
        prepare_kernel,
        out_shape=(chunked, pair, tail),
        in_specs=[HBM] * 3,
        out_specs=(VMEM,) * 3,
        scratch_shapes=[dma((parts + 4,))],
        compiler_params=params(4),
        name="prepare",
    )(*pinned(grad_output, key_states, value_states))
    grads = exchanged(chunks)
    before = passed_along(own, 2)
    apart = passed_along(last, 3, (1,))
    beside = passed_along(own, 1, (0,))
    across = core_swapped(before)
    keys, values = pl.pallas_call(
        halo_kernel,
        out_shape=(sds((window, HEAD), bf16),) * 2,
        in_specs=[VMEM] * 3,
        out_specs=(VMEM,) * 2,
        cost_estimate=cost(flops),
        compiler_params=params(4),
        name="halo",
    )(own, beside, apart)

    kept = pl.pallas_call(
        forward_kernel,
        out_shape=(
            sds((OWN * WIDE, HEAD), bf16),
            sds((OWN * HEAD, WIDE), bf16),
            sds((window, HEAD), bf16),
            sds((window, HEAD), bf16),
            sds((HEAD, window), bf16),
            sds((OWN * HEAD, WIDE), bf16),
            sds((8 * OWN, WIDE), f32),
            sds((8 * OWN, WIDE), jnp.int32),
        ),
        in_specs=[HBM, HBM] + [VMEM] * 4,
        out_specs=(VMEM,) * 8,
        scratch_shapes=[
            pltpu.SMEM(doc_start.shape, jnp.int32),
            pltpu.VMEM((SPAN, WIDE), bf16),
            pltpu.VMEM((HEAD, window), bf16),
            pltpu.VMEM((REACH * BLOCK, WIDE), f32),
            pltpu.VMEM((pairs * BLOCK, WIDE), bf16),
            dma((2,)),
        ],
        cost_estimate=cost(2 * flops, pairs * BLOCK * WIDE),
        compiler_params=params(16),
        name="forward",
    )(start_hbm, query_hbm, keys, values, before, across)

    dchunks, dnear_far, dmid, dfar, down = pl.pallas_call(
        backward_kernel,
        out_shape=(
            chunked,
            sds((SPAN + TAIL, 2 * HEAD), bf16),
            pair,
            tail,
            sds((SPAN, 2 * HEAD), f32),
        ),
        in_specs=[VMEM] * 9,
        out_specs=(VMEM,) * 5,
        scratch_shapes=[
            pltpu.VMEM((SPAN, WIDE), bf16),
            pltpu.VMEM((pairs * BLOCK, WIDE), bf16),
            pltpu.VMEM((pairs * BLOCK, WIDE), bf16),
            pltpu.VMEM((window, HEAD), f32),
            pltpu.VMEM((window, HEAD), f32),
            pltpu.VMEM((SPAN, WIDE), bf16),
        ],
        cost_estimate=cost(5 * flops, pairs * BLOCK * WIDE),
        compiler_params=params(24),
        name="backward",
    )(grads, *kept)

    back = exchanged(dchunks)
    received = core_swapped(dnear_far)
    far_back = passed_along(dfar, -3, (0,))
    merged = pl.pallas_call(
        merge_kernel,
        out_shape=pair,
        in_specs=[VMEM] * 2,
        out_specs=VMEM,
        compiler_params=params(4),
        name="merge",
    )(dmid, received)
    shifted = passed_along(merged, -2)
    folded = pl.pallas_call(
        fold_kernel,
        out_shape=sds((SPAN, 2 * HEAD), f32),
        in_specs=[VMEM] * 3,
        out_specs=VMEM,
        cost_estimate=cost(flops),
        compiler_params=params(4),
        name="fold",
    )(down, received, far_back)
    grad_key, grad_value = pl.pallas_call(
        sum_kernel,
        out_shape=(sds((SPAN, HEAD), bf16),) * 2,
        in_specs=[VMEM] * 2,
        out_specs=(HBM,) * 2,
        scratch_shapes=[pltpu.VMEM((2, SPAN, HEAD), bf16), dma((2,))],
        compiler_params=params(4),
        name="sum",
    )(folded, shifted)
    grad_query = pl.pallas_call(
        place_kernel,
        out_shape=sds((share, parts * WIDE), bf16),
        in_specs=[VMEM],
        out_specs=HBM,
        scratch_shapes=[dma((parts,))],
        compiler_params=params(4),
        name="place",
    )(back)
    return grad_query, grad_key, grad_value


def solution(mesh):
    in_specs = (
        P("ctx", "kvh"),
        P("ctx", "kvh"),
        P("ctx", "kvh"),
        P(("ctx", "kvh"), None),
        P("ctx"),
    )
    out_specs = (P(("ctx", "kvh"), None), P("ctx", "kvh"), P("ctx", "kvh"))
    return jax.shard_map(body, mesh=mesh, in_specs=in_specs, out_specs=out_specs, check_vma=False)
```

```python
import math

import jax
import jax.numpy as jnp
from jax import lax
from jax.experimental import pallas as pl
from jax.experimental.pallas import tpu as pltpu
from jax.sharding import PartitionSpec as P

HEAD = 128
GROUP = 4
BLOCK = 128
OWN = 3
REACH = 9
WINDOW = REACH + OWN - 1
WIDE = GROUP * BLOCK
SPAN = OWN * BLOCK
TAIL = 2 * BLOCK
INV_ROOT = HEAD ** (-0.5)
TO_EXP2 = INV_ROOT * math.log2(math.e)
MIB = 2**20

NT = (((1,), (1,)), ((), ()))
NN = (((1,), (0,)), ((), ()))
VMEM = pl.BlockSpec(memory_space=pltpu.VMEM)
HBM = pl.BlockSpec(memory_space=pltpu.HBM)


def dot(a, b, dims):
    return lax.dot_general(a, b, dims, preferred_element_type=jnp.float32)


def block(index, count=1):
    return slice(index * BLOCK, (index + count) * BLOCK)


def heads_stacked(value):
    return jnp.concatenate([value[:, block(h)] for h in range(GROUP)], axis=0)


def started(pairs, sems):
    copies = [pltpu.make_async_copy(a, b, sems.at[n]) for n, (a, b) in enumerate(pairs)]
    for copy in copies:
        copy.start()
    return copies


def finish(copies):
    for copy in copies:
        copy.wait()


def peer_at(position, parts):
    return lax.rem(position + lax.rem(lax.axis_index("ctx"), 2) * (parts // 2), parts)


def on_odd_core():
    return lax.rem(lax.axis_index("ctx"), 2) == 1


def peer_cols(position, parts):
    return pl.ds(pl.multiple_of(peer_at(position, parts) * WIDE, WIDE), WIDE)


def prepare_kernel(grad_hbm, key_hbm, value_hbm, chunks, pair, tail, sems):
    parts = chunks.shape[0]
    last = slice(SPAN - TAIL, SPAN)
    moves = [(grad_hbm.at[:, peer_cols(p, parts)], chunks.at[p]) for p in range(parts)]
    moves += [
        (key_hbm, pair.at[:, :HEAD]),
        (value_hbm, pair.at[:, HEAD:]),
        (key_hbm.at[last, :], tail.at[:, :HEAD]),
        (value_hbm.at[last, :], tail.at[:, HEAD:]),
    ]
    finish(started(moves, sems))


def window_of(part, far, mid, near, own):
    cols = block(part)
    return jnp.concatenate([far[:, cols], mid[:, cols], near[:, cols], own[:, cols]], axis=0)


def causal_mask():
    key_at = lax.broadcasted_iota(jnp.int32, (BLOCK, WIDE), 0)
    query_at = lax.broadcasted_iota(jnp.int32, (BLOCK, WIDE), 1) & (BLOCK - 1)
    return key_at <= query_at


def first_key():
    return lax.axis_index("ctx") * SPAN - (REACH - 1) * BLOCK


def row8(i):
    return slice(8 * i, 8 * i + 8)


def forward_kernel(
    start_hbm, query_hbm, own, near, mid, far,
    queries, key_win, value_win, attended_ref, norm_ref, starts,
    start_ref, query_ref, value_t, held, weights, sems
):
    arriving = started([(query_hbm, query_ref), (start_hbm, start_ref)], sems)
    key_win[...] = window_of(0, far, mid, near, own)
    turned_values = window_of(1, far, mid, near, own)
    value_win[...] = turned_values
    value_t[...] = turned_values.T
    causal = causal_mask()
    first = first_key()
    finish(arriving)
    for i in range(OWN):
        stacked = heads_stacked(query_ref[block(i), :])
        queries[block(i * GROUP, GROUP), :] = stacked
        turned = stacked.T
        start = start_ref[i]
        starts[row8(i), :] = jnp.full((8, WIDE), start, jnp.int32)
        best = jnp.full((8, WIDE), -jnp.inf, jnp.float32)
        for j in range(REACH):
            score = dot(key_win[block(i + j), :], turned, NN)
            allowed = causal if j == REACH - 1 else first + (i + j) * BLOCK >= start
            score = jnp.where(allowed, score, -jnp.inf)
            held[block(j), :] = score
            best = jnp.maximum(best, jnp.max(score.reshape(BLOCK // 8, 8, WIDE), axis=0))
        best = jnp.max(best, axis=0, keepdims=True)
        total = jnp.zeros((8, WIDE), jnp.float32)
        for j in range(REACH):
            part = jnp.exp2((held[block(j), :] - best) * TO_EXP2)
            total = total + jnp.sum(part.reshape(BLOCK // 8, 8, WIDE), axis=0)
            weights[block(i * REACH + j), :] = part.astype(jnp.bfloat16)
        total = jnp.sum(total, axis=0, keepdims=True)
        norm_ref[row8(i), :] = jnp.broadcast_to(best * TO_EXP2 + jnp.log2(total), (8, WIDE))
        attended_ref[block(i), :] = (
            dot(value_t[:, block(i, REACH)], weights[block(i * REACH, REACH), :], NN)
            * (1.0 / total)
        ).astype(jnp.bfloat16)


def backward_kernel(
    chunks, queries, key_win, value_win, attended_ref, norm_ref, starts,
    dchunks, dnear_far, dmid, dfar, down,
    key_t, grad_ref, weights, held, dkey, dvalue, dquery
):
    parts, share = chunks.shape[0], chunks.shape[1]

    def share_rows(p):
        return pl.ds(pl.multiple_of(peer_at(p, parts) * share, share), share)

    for p in range(parts):
        grad_ref[share_rows(p), :] = chunks[p]
    key_t[...] = key_win[...].T
    causal = causal_mask()
    first = first_key()
    on_diagonal = lax.broadcasted_iota(jnp.int32, (BLOCK, BLOCK), 0) == lax.broadcasted_iota(
        jnp.int32, (BLOCK, BLOCK), 1
    )
    for i in range(OWN):
        grads = heads_stacked(grad_ref[block(i), :])
        grads_t = grads.T
        queries_t = queries[block(i * GROUP, GROUP), :].T
        deltas = []
        for h in range(GROUP):
            cross = dot(grads[block(h), :], attended_ref[block(i), block(h)], NN)
            deltas.append(jnp.sum(jnp.where(on_diagonal, cross, 0.0), axis=0, keepdims=True))
        delta = jnp.concatenate(deltas, axis=1)
        norm = norm_ref[8 * i : 8 * i + 1, :]
        start = starts[8 * i : 8 * i + 1, :]
        for j in range(REACH):
            score = dot(key_win[block(i + j), :], queries_t, NN)
            if j == REACH - 1:
                weight = jnp.where(causal, jnp.exp2(score * TO_EXP2 - norm), 0.0)
            else:
                allowed = first + (i + j) * BLOCK >= start
                weight = jnp.exp2(score * TO_EXP2 - jnp.where(allowed, norm, jnp.inf))
            dweight = dot(value_win[block(i + j), :], grads_t, NN)
            weights[block(i * REACH + j), :] = weight.astype(jnp.bfloat16)
            held[block(i * REACH + j), :] = (weight * (dweight - delta)).astype(jnp.bfloat16)
        mine = block(i * REACH, REACH)
        turned = dot(key_t[:, block(i, REACH)], held[mine, :], NN) * INV_ROOT
        for h in range(GROUP):
            dquery[block(i), block(h)] = turned[:, block(h)].T.astype(jnp.bfloat16)
        value_part = dot(weights[mine, :], grads, NN)
        key_part = dot(held[mine, :], queries[block(i * GROUP, GROUP), :], NN)
        fresh = 0 if i == 0 else REACH - 1
        if fresh:
            seen = slice(0, fresh * BLOCK)
            dvalue[block(i, fresh), :] += value_part[seen, :]
            dkey[block(i, fresh), :] += key_part[seen, :]
        rest = slice(fresh * BLOCK, REACH * BLOCK)
        dvalue[block(i + fresh, REACH - fresh), :] = value_part[rest, :]
        dkey[block(i + fresh, REACH - fresh), :] = key_part[rest, :]
    for p in range(parts):
        dchunks[p] = dquery[share_rows(p), :]

    def put(ref, at, lo, count):
        to, span = slice(at, at + count), slice(lo, lo + count)
        ref[to, :HEAD] = (dkey[span, :] * INV_ROOT).astype(ref.dtype)
        ref[to, HEAD:] = dvalue[span, :].astype(ref.dtype)

    put(dnear_far, 0, TAIL + SPAN, SPAN)
    put(dnear_far, SPAN, 0, TAIL)
    put(dfar, 0, 0, TAIL)
    put(dmid, 0, TAIL, SPAN)
    put(down, 0, TAIL + 2 * SPAN, SPAN)


def merge_kernel(dmid, received, merged):
    odd = on_odd_core()
    f32 = jnp.float32

    @pl.when(odd)
    def _():
        merged[...] = (dmid[...].astype(f32) + received[:SPAN, :].astype(f32)).astype(merged.dtype)

    @pl.when(jnp.logical_not(odd))
    def _():
        head, last = slice(0, SPAN - TAIL), slice(SPAN - TAIL, SPAN)
        merged[head, :] = dmid[head, :]
        merged[last, :] = (
            dmid[last, :].astype(f32) + received[SPAN:, :].astype(f32)
        ).astype(merged.dtype)


def fold_kernel(down, received, apart, folded):
    odd = on_odd_core()
    f32 = jnp.float32

    @pl.when(odd)
    def _():
        head, last = slice(0, SPAN - TAIL), slice(SPAN - TAIL, SPAN)
        folded[head, :] = down[head, :]
        folded[last, :] = down[last, :] + apart[...].astype(f32)

    @pl.when(jnp.logical_not(odd))
    def _():
        folded[...] = down[...] + received[:SPAN, :].astype(f32)


def sum_kernel(folded, shifted, key_hbm, value_hbm, out, sems):
    total = folded[...] + shifted[...].astype(jnp.float32)
    for part in range(2):
        out[part] = total[:, block(part)].astype(out.dtype)
    finish(started([(out.at[0], key_hbm), (out.at[1], value_hbm)], sems))


def place_kernel(chunks, out_hbm, sems):
    parts = chunks.shape[0]
    finish(
        started([(chunks.at[p], out_hbm.at[:, peer_cols(p, parts)]) for p in range(parts)], sems)
    )


def passed_along(value, by, parities=(0, 1)):
    length = lax.axis_size("ctx")
    pairs = [
        (i, i + by) for i in range(length) if 0 <= i + by < length and i % 2 in parities
    ]
    return lax.ppermute(value, "ctx", pairs)


def core_swapped(value):
    return lax.ppermute(value, "ctx", [(i, i ^ 1) for i in range(lax.axis_size("ctx"))])


def pinned(*arrays):
    return [pltpu.with_memory_space_constraint(x, pltpu.HBM) for x in arrays]


def cost(flops, exps=0):
    return pl.CostEstimate(flops=int(flops), bytes_accessed=8 * MIB, transcendentals=int(exps))


def params(mib):
    return pltpu.CompilerParams(vmem_limit_bytes=mib * MIB)


def body(query_states, key_states, value_states, grad_output, doc_start):
    parts, length = lax.axis_size("kvh"), lax.axis_size("ctx")
    share = SPAN // parts
    bf16, f32 = jnp.bfloat16, jnp.float32
    sds = jax.ShapeDtypeStruct
    dma = pltpu.SemaphoreType.DMA
    window = WINDOW * BLOCK
    pairs = OWN * REACH
    flops = 2 * pairs * BLOCK * BLOCK * WIDE
    chunked = sds((parts, share, WIDE), bf16)
    pair = sds((SPAN, 2 * HEAD), bf16)
    tail = sds((TAIL, 2 * HEAD), bf16)
    rings = [
        [c * parts + (p + (c % 2) * (parts // 2)) % parts for p in range(parts)]
        for c in range(length)
    ]

    def exchanged(value):
        return lax.all_to_all(
            value, ("ctx", "kvh"), split_axis=0, concat_axis=0, axis_index_groups=rings, tiled=True
        )

    start_hbm, query_hbm = pinned(doc_start, query_states)
    chunks, own, last = pl.pallas_call(
        prepare_kernel,
        out_shape=(chunked, pair, tail),
        in_specs=[HBM] * 3,
        out_specs=(VMEM,) * 3,
        scratch_shapes=[dma((parts + 4,))],
        compiler_params=params(4),
        name="prepare",
    )(*pinned(grad_output, key_states, value_states))
    grads = exchanged(chunks)
    far = passed_along(last, 3)
    mid = passed_along(own, 2)
    near = passed_along(own, 1)

    kept = pl.pallas_call(
        forward_kernel,
        out_shape=(
            sds((OWN * WIDE, HEAD), bf16),
            sds((window, HEAD), bf16),
            sds((window, HEAD), bf16),
            sds((OWN * HEAD, WIDE), bf16),
            sds((8 * OWN, WIDE), f32),
            sds((8 * OWN, WIDE), jnp.int32),
        ),
        in_specs=[HBM, HBM] + [VMEM] * 4,
        out_specs=(VMEM,) * 6,
        scratch_shapes=[
            pltpu.SMEM(doc_start.shape, jnp.int32),
            pltpu.VMEM((SPAN, WIDE), bf16),
            pltpu.VMEM((HEAD, window), bf16),
            pltpu.VMEM((REACH * BLOCK, WIDE), f32),
            pltpu.VMEM((pairs * BLOCK, WIDE), bf16),
            dma((2,)),
        ],
        cost_estimate=cost(2 * flops, pairs * BLOCK * WIDE),
        compiler_params=params(16),
        name="forward",
    )(start_hbm, query_hbm, own, near, mid, far)

    dchunks, dnear_far, dmid, dfar, down = pl.pallas_call(
        backward_kernel,
        out_shape=(
            chunked,
            sds((SPAN + TAIL, 2 * HEAD), bf16),
            pair,
            tail,
            sds((SPAN, 2 * HEAD), f32),
        ),
        in_specs=[VMEM] * 7,
        out_specs=(VMEM,) * 5,
        scratch_shapes=[
            pltpu.VMEM((HEAD, window), bf16),
            pltpu.VMEM((SPAN, WIDE), bf16),
            pltpu.VMEM((pairs * BLOCK, WIDE), bf16),
            pltpu.VMEM((pairs * BLOCK, WIDE), bf16),
            pltpu.VMEM((window, HEAD), f32),
            pltpu.VMEM((window, HEAD), f32),
            pltpu.VMEM((SPAN, WIDE), bf16),
        ],
        cost_estimate=cost(5 * flops, pairs * BLOCK * WIDE),
        compiler_params=params(24),
        name="backward",
    )(grads, *kept)

    back = exchanged(dchunks)
    received = core_swapped(dnear_far)
    far_back = passed_along(dfar, -3, (0,))
    merged = pl.pallas_call(
        merge_kernel,
        out_shape=pair,
        in_specs=[VMEM] * 2,
        out_specs=VMEM,
        compiler_params=params(4),
        name="merge",
    )(dmid, received)
    shifted = passed_along(merged, -2)
    folded = pl.pallas_call(
        fold_kernel,
        out_shape=sds((SPAN, 2 * HEAD), f32),
        in_specs=[VMEM] * 3,
        out_specs=VMEM,
        cost_estimate=cost(flops),
        compiler_params=params(4),
        name="fold",
    )(down, received, far_back)
    grad_key, grad_value = pl.pallas_call(
        sum_kernel,
        out_shape=(sds((SPAN, HEAD), bf16),) * 2,
        in_specs=[VMEM] * 2,
        out_specs=(HBM,) * 2,
        scratch_shapes=[pltpu.VMEM((2, SPAN, HEAD), bf16), dma((2,))],
        compiler_params=params(4),
        name="sum",
    )(folded, shifted)
    grad_query = pl.pallas_call(
        place_kernel,
        out_shape=sds((share, parts * WIDE), bf16),
        in_specs=[VMEM],
        out_specs=HBM,
        scratch_shapes=[dma((parts,))],
        compiler_params=params(4),
        name="place",
    )(back)
    return grad_query, grad_key, grad_value


def solution(mesh):
    in_specs = (
        P("ctx", "kvh"),
        P("ctx", "kvh"),
        P("ctx", "kvh"),
        P(("ctx", "kvh"), None),
        P("ctx"),
    )
    out_specs = (P(("ctx", "kvh"), None), P("ctx", "kvh"), P("ctx", "kvh"))
    return jax.shard_map(body, mesh=mesh, in_specs=in_specs, out_specs=out_specs, check_vma=False)
```

```python
import math

import jax
import jax.numpy as jnp
from jax import lax
from jax.experimental import pallas as pl
from jax.experimental.pallas import tpu as pltpu
from jax.sharding import PartitionSpec as P

HEAD = 128
GROUP = 4
BLOCK = 128
OWN = 3
REACH = 9
WINDOW = REACH + OWN - 1
WIDE = GROUP * BLOCK
SPAN = OWN * BLOCK
TAIL = 2 * BLOCK
INV_ROOT = HEAD ** (-0.5)
TO_EXP2 = INV_ROOT * math.log2(math.e)
MIB = 2**20

NT = (((1,), (1,)), ((), ()))
NN = (((1,), (0,)), ((), ()))
VMEM = pl.BlockSpec(memory_space=pltpu.VMEM)
HBM = pl.BlockSpec(memory_space=pltpu.HBM)


def dot(a, b, dims):
    return lax.dot_general(a, b, dims, preferred_element_type=jnp.float32)


def block(index, count=1):
    return slice(index * BLOCK, (index + count) * BLOCK)


def heads_stacked(value):
    return jnp.concatenate([value[:, block(h)] for h in range(GROUP)], axis=0)


def started(pairs, sems):
    copies = [pltpu.make_async_copy(a, b, sems.at[n]) for n, (a, b) in enumerate(pairs)]
    for copy in copies:
        copy.start()
    return copies


def finish(copies):
    for copy in copies:
        copy.wait()


def peer_at(position, parts):
    return lax.rem(position + lax.rem(lax.axis_index("ctx"), 2) * (parts // 2), parts)


def on_odd_core():
    return lax.rem(lax.axis_index("ctx"), 2) == 1


def peer_cols(position, parts):
    return pl.ds(pl.multiple_of(peer_at(position, parts) * WIDE, WIDE), WIDE)


def prepare_kernel(grad_hbm, key_hbm, value_hbm, chunks, pair, tail, sems):
    parts = chunks.shape[0]
    last = slice(SPAN - TAIL, SPAN)
    moves = [(grad_hbm.at[:, peer_cols(p, parts)], chunks.at[p]) for p in range(parts)]
    moves += [
        (key_hbm, pair.at[:, :HEAD]),
        (value_hbm, pair.at[:, HEAD:]),
        (key_hbm.at[last, :], tail.at[:, :HEAD]),
        (value_hbm.at[last, :], tail.at[:, HEAD:]),
    ]
    finish(started(moves, sems))


def later_kernel(own, later):
    later[...] = own[...]


def window_of(part, far, mid, near, own):
    cols = block(part)
    return jnp.concatenate([far[:, cols], mid[:, cols], near[:, cols], own[:, cols]], axis=0)


def causal_mask():
    key_at = lax.broadcasted_iota(jnp.int32, (BLOCK, WIDE), 0)
    query_at = lax.broadcasted_iota(jnp.int32, (BLOCK, WIDE), 1) & (BLOCK - 1)
    return key_at <= query_at


def first_key():
    return lax.axis_index("ctx") * SPAN - (REACH - 1) * BLOCK


def row8(i):
    return slice(8 * i, 8 * i + 8)


def forward_kernel(
    start_hbm, query_hbm, own, near, mid, far,
    queries, key_win, value_win, attended_ref, norm_ref, starts,
    start_ref, query_ref, value_t, held, weights, sems
):
    arriving = started([(query_hbm, query_ref), (start_hbm, start_ref)], sems)
    key_win[...] = window_of(0, far, mid, near, own)
    turned_values = window_of(1, far, mid, near, own)
    value_win[...] = turned_values
    value_t[...] = turned_values.T
    causal = causal_mask()
    first = first_key()
    finish(arriving)
    for i in range(OWN):
        stacked = heads_stacked(query_ref[block(i), :])
        queries[block(i * GROUP, GROUP), :] = stacked
        turned = stacked.T
        start = start_ref[i]
        starts[row8(i), :] = jnp.full((8, WIDE), start, jnp.int32)
        best = jnp.full((8, WIDE), -jnp.inf, jnp.float32)
        for j in range(REACH):
            score = dot(key_win[block(i + j), :], turned, NN)
            allowed = causal if j == REACH - 1 else first + (i + j) * BLOCK >= start
            score = jnp.where(allowed, score, -jnp.inf)
            held[block(j), :] = score
            best = jnp.maximum(best, jnp.max(score.reshape(BLOCK // 8, 8, WIDE), axis=0))
        best = jnp.max(best, axis=0, keepdims=True)
        total = jnp.zeros((8, WIDE), jnp.float32)
        for j in range(REACH):
            part = jnp.exp2((held[block(j), :] - best) * TO_EXP2)
            total = total + jnp.sum(part.reshape(BLOCK // 8, 8, WIDE), axis=0)
            weights[block(i * REACH + j), :] = part.astype(jnp.bfloat16)
        total = jnp.sum(total, axis=0, keepdims=True)
        norm_ref[row8(i), :] = jnp.broadcast_to(best * TO_EXP2 + jnp.log2(total), (8, WIDE))
        attended_ref[block(i), :] = (
            dot(value_t[:, block(i, REACH)], weights[block(i * REACH, REACH), :], NN)
            * (1.0 / total)
        ).astype(jnp.bfloat16)


def backward_kernel(
    chunks, queries, key_win, value_win, attended_ref, norm_ref, starts,
    dchunks, dnear_far, dmid, dfar, down,
    key_t, grad_ref, weights, held, dkey, dvalue, dquery
):
    parts, share = chunks.shape[0], chunks.shape[1]

    def share_rows(p):
        return pl.ds(pl.multiple_of(peer_at(p, parts) * share, share), share)

    for p in range(parts):
        grad_ref[share_rows(p), :] = chunks[p]
    key_t[...] = key_win[...].T
    causal = causal_mask()
    first = first_key()
    on_diagonal = lax.broadcasted_iota(jnp.int32, (BLOCK, BLOCK), 0) == lax.broadcasted_iota(
        jnp.int32, (BLOCK, BLOCK), 1
    )
    for i in range(OWN):
        grads = heads_stacked(grad_ref[block(i), :])
        grads_t = grads.T
        queries_t = queries[block(i * GROUP, GROUP), :].T
        deltas = []
        for h in range(GROUP):
            cross = dot(grads[block(h), :], attended_ref[block(i), block(h)], NN)
            deltas.append(jnp.sum(jnp.where(on_diagonal, cross, 0.0), axis=0, keepdims=True))
        delta = jnp.concatenate(deltas, axis=1)
        norm = norm_ref[8 * i : 8 * i + 1, :]
        start = starts[8 * i : 8 * i + 1, :]
        for j in range(REACH):
            score = dot(key_win[block(i + j), :], queries_t, NN)
            if j == REACH - 1:
                weight = jnp.where(causal, jnp.exp2(score * TO_EXP2 - norm), 0.0)
            else:
                allowed = first + (i + j) * BLOCK >= start
                weight = jnp.exp2(score * TO_EXP2 - jnp.where(allowed, norm, jnp.inf))
            dweight = dot(value_win[block(i + j), :], grads_t, NN)
            weights[block(i * REACH + j), :] = weight.astype(jnp.bfloat16)
            held[block(i * REACH + j), :] = (weight * (dweight - delta)).astype(jnp.bfloat16)
        mine = block(i * REACH, REACH)
        turned = dot(key_t[:, block(i, REACH)], held[mine, :], NN) * INV_ROOT
        for h in range(GROUP):
            dquery[block(i), block(h)] = turned[:, block(h)].T.astype(jnp.bfloat16)
        value_part = dot(weights[mine, :], grads, NN)
        key_part = dot(held[mine, :], queries[block(i * GROUP, GROUP), :], NN)
        fresh = 0 if i == 0 else REACH - 1
        if fresh:
            seen = slice(0, fresh * BLOCK)
            dvalue[block(i, fresh), :] += value_part[seen, :]
            dkey[block(i, fresh), :] += key_part[seen, :]
        rest = slice(fresh * BLOCK, REACH * BLOCK)
        dvalue[block(i + fresh, REACH - fresh), :] = value_part[rest, :]
        dkey[block(i + fresh, REACH - fresh), :] = key_part[rest, :]
    for p in range(parts):
        dchunks[p] = dquery[share_rows(p), :]

    def put(ref, at, lo, count):
        to, span = slice(at, at + count), slice(lo, lo + count)
        ref[to, :HEAD] = (dkey[span, :] * INV_ROOT).astype(ref.dtype)
        ref[to, HEAD:] = dvalue[span, :].astype(ref.dtype)

    put(dnear_far, 0, TAIL + SPAN, SPAN)
    put(dnear_far, SPAN, 0, TAIL)
    put(dfar, 0, 0, TAIL)
    put(dmid, 0, TAIL, SPAN)
    put(down, 0, TAIL + 2 * SPAN, SPAN)


def merge_kernel(dmid, received, merged):
    odd = on_odd_core()
    f32 = jnp.float32

    @pl.when(odd)
    def _():
        merged[...] = (dmid[...].astype(f32) + received[:SPAN, :].astype(f32)).astype(merged.dtype)

    @pl.when(jnp.logical_not(odd))
    def _():
        head, last = slice(0, SPAN - TAIL), slice(SPAN - TAIL, SPAN)
        merged[head, :] = dmid[head, :]
        merged[last, :] = (
            dmid[last, :].astype(f32) + received[SPAN:, :].astype(f32)
        ).astype(merged.dtype)


def fold_kernel(down, received, apart, folded):
    odd = on_odd_core()
    f32 = jnp.float32

    @pl.when(odd)
    def _():
        head, last = slice(0, SPAN - TAIL), slice(SPAN - TAIL, SPAN)
        folded[head, :] = down[head, :]
        folded[last, :] = down[last, :] + apart[...].astype(f32)

    @pl.when(jnp.logical_not(odd))
    def _():
        folded[...] = down[...] + received[:SPAN, :].astype(f32)


def sum_kernel(folded, shifted, key_hbm, value_hbm, out, sems):
    total = folded[...] + shifted[...].astype(jnp.float32)
    for part in range(2):
        out[part] = total[:, block(part)].astype(out.dtype)
    finish(started([(out.at[0], key_hbm), (out.at[1], value_hbm)], sems))


def place_kernel(chunks, out_hbm, sems):
    parts = chunks.shape[0]
    finish(
        started([(chunks.at[p], out_hbm.at[:, peer_cols(p, parts)]) for p in range(parts)], sems)
    )


def passed_along(value, by, parities=(0, 1)):
    length = lax.axis_size("ctx")
    pairs = [
        (i, i + by) for i in range(length) if 0 <= i + by < length and i % 2 in parities
    ]
    return lax.ppermute(value, "ctx", pairs)


def core_swapped(value):
    return lax.ppermute(value, "ctx", [(i, i ^ 1) for i in range(lax.axis_size("ctx"))])


def pinned(*arrays):
    return [pltpu.with_memory_space_constraint(x, pltpu.HBM) for x in arrays]


def cost(flops, exps=0):
    return pl.CostEstimate(flops=int(flops), bytes_accessed=8 * MIB, transcendentals=int(exps))


def params(mib):
    return pltpu.CompilerParams(vmem_limit_bytes=mib * MIB)


def body(query_states, key_states, value_states, grad_output, doc_start):
    parts, length = lax.axis_size("kvh"), lax.axis_size("ctx")
    share = SPAN // parts
    bf16, f32 = jnp.bfloat16, jnp.float32
    sds = jax.ShapeDtypeStruct
    dma = pltpu.SemaphoreType.DMA
    window = WINDOW * BLOCK
    pairs = OWN * REACH
    flops = 2 * pairs * BLOCK * BLOCK * WIDE
    chunked = sds((parts, share, WIDE), bf16)
    pair = sds((SPAN, 2 * HEAD), bf16)
    tail = sds((TAIL, 2 * HEAD), bf16)
    rings = [
        [c * parts + (p + (c % 2) * (parts // 2)) % parts for p in range(parts)]
        for c in range(length)
    ]

    def exchanged(value):
        return lax.all_to_all(
            value, ("ctx", "kvh"), split_axis=0, concat_axis=0, axis_index_groups=rings, tiled=True
        )

    start_hbm, query_hbm = pinned(doc_start, query_states)
    chunks, own, last = pl.pallas_call(
        prepare_kernel,
        out_shape=(chunked, pair, tail),
        in_specs=[HBM] * 3,
        out_specs=(VMEM,) * 3,
        scratch_shapes=[dma((parts + 4,))],
        compiler_params=params(4),
        name="prepare",
    )(*pinned(grad_output, key_states, value_states))
    grads = exchanged(chunks)
    far = passed_along(last, 3)
    own = pl.pallas_call(
        later_kernel,
        out_shape=pair,
        in_specs=[VMEM],
        out_specs=VMEM,
        cost_estimate=cost(12 * flops),
        compiler_params=params(4),
        name="later",
    )(own)
    mid = passed_along(own, 2)
    near = passed_along(own, 1)

    kept = pl.pallas_call(
        forward_kernel,
        out_shape=(
            sds((OWN * WIDE, HEAD), bf16),
            sds((window, HEAD), bf16),
            sds((window, HEAD), bf16),
            sds((OWN * HEAD, WIDE), bf16),
            sds((8 * OWN, WIDE), f32),
            sds((8 * OWN, WIDE), jnp.int32),
        ),
        in_specs=[HBM, HBM] + [VMEM] * 4,
        out_specs=(VMEM,) * 6,
        scratch_shapes=[
            pltpu.SMEM(doc_start.shape, jnp.int32),
            pltpu.VMEM((SPAN, WIDE), bf16),
            pltpu.VMEM((HEAD, window), bf16),
            pltpu.VMEM((REACH * BLOCK, WIDE), f32),
            pltpu.VMEM((pairs * BLOCK, WIDE), bf16),
            dma((2,)),
        ],
        cost_estimate=cost(2 * flops, pairs * BLOCK * WIDE),
        compiler_params=params(16),
        name="forward",
    )(start_hbm, query_hbm, own, near, mid, far)

    dchunks, dnear_far, dmid, dfar, down = pl.pallas_call(
        backward_kernel,
        out_shape=(
            chunked,
            sds((SPAN + TAIL, 2 * HEAD), bf16),
            pair,
            tail,
            sds((SPAN, 2 * HEAD), f32),
        ),
        in_specs=[VMEM] * 7,
        out_specs=(VMEM,) * 5,
        scratch_shapes=[
            pltpu.VMEM((HEAD, window), bf16),
            pltpu.VMEM((SPAN, WIDE), bf16),
            pltpu.VMEM((pairs * BLOCK, WIDE), bf16),
            pltpu.VMEM((pairs * BLOCK, WIDE), bf16),
            pltpu.VMEM((window, HEAD), f32),
            pltpu.VMEM((window, HEAD), f32),
            pltpu.VMEM((SPAN, WIDE), bf16),
        ],
        cost_estimate=cost(5 * flops, pairs * BLOCK * WIDE),
        compiler_params=params(24),
        name="backward",
    )(grads, *kept)

    back = exchanged(dchunks)
    received = core_swapped(dnear_far)
    far_back = passed_along(dfar, -3, (0,))
    merged = pl.pallas_call(
        merge_kernel,
        out_shape=pair,
        in_specs=[VMEM] * 2,
        out_specs=VMEM,
        compiler_params=params(4),
        name="merge",
    )(dmid, received)
    shifted = passed_along(merged, -2)
    folded = pl.pallas_call(
        fold_kernel,
        out_shape=sds((SPAN, 2 * HEAD), f32),
        in_specs=[VMEM] * 3,
        out_specs=VMEM,
        cost_estimate=cost(12 * flops),
        compiler_params=params(4),
        name="fold",
    )(down, received, far_back)
    grad_key, grad_value = pl.pallas_call(
        sum_kernel,
        out_shape=(sds((SPAN, HEAD), bf16),) * 2,
        in_specs=[VMEM] * 2,
        out_specs=(HBM,) * 2,
        scratch_shapes=[pltpu.VMEM((2, SPAN, HEAD), bf16), dma((2,))],
        compiler_params=params(4),
        name="sum",
    )(folded, shifted)
    grad_query = pl.pallas_call(
        place_kernel,
        out_shape=sds((share, parts * WIDE), bf16),
        in_specs=[VMEM],
        out_specs=HBM,
        scratch_shapes=[dma((parts,))],
        compiler_params=params(4),
        name="place",
    )(back)
    return grad_query, grad_key, grad_value


def solution(mesh):
    in_specs = (
        P("ctx", "kvh"),
        P("ctx", "kvh"),
        P("ctx", "kvh"),
        P(("ctx", "kvh"), None),
        P("ctx"),
    )
    out_specs = (P(("ctx", "kvh"), None), P("ctx", "kvh"), P("ctx", "kvh"))
    return jax.shard_map(body, mesh=mesh, in_specs=in_specs, out_specs=out_specs, check_vma=False)
```

```python
import math

import jax
import jax.numpy as jnp
from jax import lax
from jax.experimental import pallas as pl
from jax.experimental.pallas import tpu as pltpu
from jax.sharding import PartitionSpec as P

HEAD = 128
GROUP = 4
BLOCK = 128
OWN = 3
REACH = 9
WINDOW = REACH + OWN - 1
WIDE = GROUP * BLOCK
SPAN = OWN * BLOCK
TAIL = 2 * BLOCK
INV_ROOT = HEAD ** (-0.5)
TO_EXP2 = INV_ROOT * math.log2(math.e)
MIB = 2**20

NT = (((1,), (1,)), ((), ()))
NN = (((1,), (0,)), ((), ()))
VMEM = pl.BlockSpec(memory_space=pltpu.VMEM)
HBM = pl.BlockSpec(memory_space=pltpu.HBM)


def dot(a, b, dims):
    return lax.dot_general(a, b, dims, preferred_element_type=jnp.float32)


def block(index, count=1):
    return slice(index * BLOCK, (index + count) * BLOCK)


def heads_stacked(value):
    return jnp.concatenate([value[:, block(h)] for h in range(GROUP)], axis=0)


def started(pairs, sems):
    copies = [pltpu.make_async_copy(a, b, sems.at[n]) for n, (a, b) in enumerate(pairs)]
    for copy in copies:
        copy.start()
    return copies


def finish(copies):
    for copy in copies:
        copy.wait()


def peer_at(position, parts):
    return lax.rem(position + lax.rem(lax.axis_index("ctx"), 2) * (parts // 2), parts)


def on_odd_core():
    return lax.rem(lax.axis_index("ctx"), 2) == 1


def peer_cols(position, parts):
    return pl.ds(pl.multiple_of(peer_at(position, parts) * WIDE, WIDE), WIDE)


def prepare_kernel(
    start_hbm, query_hbm, grad_hbm, key_hbm, value_hbm,
    chunks, pair, tail, query, starts, start_ref, sems
):
    parts = chunks.shape[0]
    last = slice(SPAN - TAIL, SPAN)
    moves = [(start_hbm, start_ref)]
    moves += [(grad_hbm.at[:, peer_cols(p, parts)], chunks.at[p]) for p in range(parts)]
    moves += [
        (key_hbm, pair.at[:, :HEAD]),
        (value_hbm, pair.at[:, HEAD:]),
        (key_hbm.at[last, :], tail.at[:, :HEAD]),
        (value_hbm.at[last, :], tail.at[:, HEAD:]),
        (query_hbm, query),
    ]
    copies = started(moves, sems)
    finish(copies[:1])
    for i in range(OWN):
        starts[row8(i), :] = jnp.full((8, WIDE), start_ref[i], jnp.int32)
    finish(copies[1:])


def later_kernel(own, later):
    later[...] = own[...]


def window_of(part, far, mid, near, own):
    cols = block(part)
    return jnp.concatenate([far[:, cols], mid[:, cols], near[:, cols], own[:, cols]], axis=0)


def causal_mask():
    key_at = lax.broadcasted_iota(jnp.int32, (BLOCK, WIDE), 0)
    query_at = lax.broadcasted_iota(jnp.int32, (BLOCK, WIDE), 1) & (BLOCK - 1)
    return key_at <= query_at


def first_key():
    return lax.axis_index("ctx") * SPAN - (REACH - 1) * BLOCK


def row8(i):
    return slice(8 * i, 8 * i + 8)


def attention_kernel(
    chunks, query_ref, starts, own, near, mid, far,
    dchunks, dnear_far, dmid, dfar, down,
    key_win, value_win, value_t, key_t, scores, grad_ref, weights, held, dkey, dvalue, dquery
):
    parts, share = chunks.shape[0], chunks.shape[1]

    def share_rows(p):
        return pl.ds(pl.multiple_of(peer_at(p, parts) * share, share), share)

    for p in range(parts):
        grad_ref[share_rows(p), :] = chunks[p]
    keys = window_of(0, far, mid, near, own)
    key_win[...] = keys
    key_t[...] = keys.T
    values = window_of(1, far, mid, near, own)
    value_win[...] = values
    value_t[...] = values.T
    causal = causal_mask()
    first = first_key()
    on_diagonal = lax.broadcasted_iota(jnp.int32, (BLOCK, BLOCK), 0) == lax.broadcasted_iota(
        jnp.int32, (BLOCK, BLOCK), 1
    )
    for i in range(OWN):
        mine = block(i * REACH, REACH)
        queries = heads_stacked(query_ref[block(i), :])
        queries_t = queries.T
        start = starts[8 * i : 8 * i + 1, :]
        best = jnp.full((8, WIDE), -jnp.inf, jnp.float32)
        for j in range(REACH):
            score = dot(key_win[block(i + j), :], queries_t, NN)
            allowed = causal if j == REACH - 1 else first + (i + j) * BLOCK >= start
            score = jnp.where(allowed, score, -jnp.inf)
            scores[block(i * REACH + j), :] = score
            best = jnp.maximum(best, jnp.max(score.reshape(BLOCK // 8, 8, WIDE), axis=0))
        best = jnp.max(best, axis=0, keepdims=True)
        total = jnp.zeros((8, WIDE), jnp.float32)
        for j in range(REACH):
            part = jnp.exp2((scores[block(i * REACH + j), :] - best) * TO_EXP2)
            total = total + jnp.sum(part.reshape(BLOCK // 8, 8, WIDE), axis=0)
            weights[block(i * REACH + j), :] = part.astype(jnp.bfloat16)
        inverse = 1.0 / jnp.sum(total, axis=0, keepdims=True)
        attended = (
            dot(value_t[:, block(i, REACH)], weights[mine, :], NN) * inverse
        ).astype(jnp.bfloat16)
        per_row = jnp.concatenate(
            [jnp.broadcast_to(inverse[:, block(h)], (BLOCK, BLOCK)).T for h in range(GROUP)], axis=0
        )
        grads = (heads_stacked(grad_ref[block(i), :]).astype(jnp.float32) * per_row).astype(
            jnp.bfloat16
        )
        grads_t = grads.T
        deltas = []
        for h in range(GROUP):
            cross = dot(grads[block(h), :], attended[:, block(h)], NN)
            deltas.append(jnp.sum(jnp.where(on_diagonal, cross, 0.0), axis=0, keepdims=True))
        delta = jnp.concatenate(deltas, axis=1)
        for j in range(REACH):
            dweight = dot(value_win[block(i + j), :], grads_t, NN)
            weight = weights[block(i * REACH + j), :].astype(jnp.float32)
            held[block(i * REACH + j), :] = (weight * (dweight - delta)).astype(jnp.bfloat16)
        turned = dot(key_t[:, block(i, REACH)], held[mine, :], NN) * INV_ROOT
        for h in range(GROUP):
            dquery[block(i), block(h)] = turned[:, block(h)].T.astype(jnp.bfloat16)
        value_part = dot(weights[mine, :], grads, NN)
        key_part = dot(held[mine, :], queries, NN)
        fresh = 0 if i == 0 else REACH - 1
        if fresh:
            seen = slice(0, fresh * BLOCK)
            dvalue[block(i, fresh), :] += value_part[seen, :]
            dkey[block(i, fresh), :] += key_part[seen, :]
        rest = slice(fresh * BLOCK, REACH * BLOCK)
        dvalue[block(i + fresh, REACH - fresh), :] = value_part[rest, :]
        dkey[block(i + fresh, REACH - fresh), :] = key_part[rest, :]
    for p in range(parts):
        dchunks[p] = dquery[share_rows(p), :]

    def put(ref, at, lo, count):
        to, span = slice(at, at + count), slice(lo, lo + count)
        ref[to, :HEAD] = (dkey[span, :] * INV_ROOT).astype(ref.dtype)
        ref[to, HEAD:] = dvalue[span, :].astype(ref.dtype)

    put(dnear_far, 0, TAIL + SPAN, SPAN)
    put(dnear_far, SPAN, 0, TAIL)
    put(dfar, 0, 0, TAIL)
    put(dmid, 0, TAIL, SPAN)
    put(down, 0, TAIL + 2 * SPAN, SPAN)


def merge_kernel(dmid, received, merged):
    odd = on_odd_core()
    f32 = jnp.float32

    @pl.when(odd)
    def _():
        merged[...] = (dmid[...].astype(f32) + received[:SPAN, :].astype(f32)).astype(merged.dtype)

    @pl.when(jnp.logical_not(odd))
    def _():
        head, last = slice(0, SPAN - TAIL), slice(SPAN - TAIL, SPAN)
        merged[head, :] = dmid[head, :]
        merged[last, :] = (
            dmid[last, :].astype(f32) + received[SPAN:, :].astype(f32)
        ).astype(merged.dtype)


def fold_kernel(down, received, apart, folded):
    odd = on_odd_core()
    f32 = jnp.float32

    @pl.when(odd)
    def _():
        head, last = slice(0, SPAN - TAIL), slice(SPAN - TAIL, SPAN)
        folded[head, :] = down[head, :]
        folded[last, :] = down[last, :] + apart[...].astype(f32)

    @pl.when(jnp.logical_not(odd))
    def _():
        folded[...] = down[...] + received[:SPAN, :].astype(f32)


def sum_kernel(folded, shifted, key_hbm, value_hbm, out, sems):
    total = folded[...] + shifted[...].astype(jnp.float32)
    for part in range(2):
        out[part] = total[:, block(part)].astype(out.dtype)
    finish(started([(out.at[0], key_hbm), (out.at[1], value_hbm)], sems))


def place_kernel(chunks, out_hbm, sems):
    parts = chunks.shape[0]
    finish(
        started([(chunks.at[p], out_hbm.at[:, peer_cols(p, parts)]) for p in range(parts)], sems)
    )


def passed_along(value, by, parities=(0, 1)):
    length = lax.axis_size("ctx")
    pairs = [
        (i, i + by) for i in range(length) if 0 <= i + by < length and i % 2 in parities
    ]
    return lax.ppermute(value, "ctx", pairs)


def core_swapped(value):
    return lax.ppermute(value, "ctx", [(i, i ^ 1) for i in range(lax.axis_size("ctx"))])


def pinned(*arrays):
    return [pltpu.with_memory_space_constraint(x, pltpu.HBM) for x in arrays]


def cost(flops, exps=0):
    return pl.CostEstimate(flops=int(flops), bytes_accessed=8 * MIB, transcendentals=int(exps))


def params(mib):
    return pltpu.CompilerParams(vmem_limit_bytes=mib * MIB)


def body(query_states, key_states, value_states, grad_output, doc_start):
    parts, length = lax.axis_size("kvh"), lax.axis_size("ctx")
    share = SPAN // parts
    bf16, f32 = jnp.bfloat16, jnp.float32
    sds = jax.ShapeDtypeStruct
    dma = pltpu.SemaphoreType.DMA
    window = WINDOW * BLOCK
    pairs = OWN * REACH
    flops = 2 * pairs * BLOCK * BLOCK * WIDE
    chunked = sds((parts, share, WIDE), bf16)
    pair = sds((SPAN, 2 * HEAD), bf16)
    tail = sds((TAIL, 2 * HEAD), bf16)
    rings = [
        [c * parts + (p + (c % 2) * (parts // 2)) % parts for p in range(parts)]
        for c in range(length)
    ]

    def exchanged(value):
        return lax.all_to_all(
            value, ("ctx", "kvh"), split_axis=0, concat_axis=0, axis_index_groups=rings, tiled=True
        )

    chunks, own, last, queries, starts = pl.pallas_call(
        prepare_kernel,
        out_shape=(
            chunked, pair, tail, sds((SPAN, WIDE), bf16), sds((8 * OWN, WIDE), jnp.int32)
        ),
        in_specs=[HBM] * 5,
        out_specs=(VMEM,) * 5,
        scratch_shapes=[pltpu.SMEM(doc_start.shape, jnp.int32), dma((parts + 6,))],
        compiler_params=params(4),
        name="prepare",
    )(*pinned(doc_start, query_states, grad_output, key_states, value_states))
    grads = exchanged(chunks)
    far = passed_along(last, 3)
    own = pl.pallas_call(
        later_kernel,
        out_shape=pair,
        in_specs=[VMEM],
        out_specs=VMEM,
        cost_estimate=cost(12 * flops),
        compiler_params=params(4),
        name="later",
    )(own)
    mid = passed_along(own, 2)
    near = passed_along(own, 1)

    dchunks, dnear_far, dmid, dfar, down = pl.pallas_call(
        attention_kernel,
        out_shape=(
            chunked,
            sds((SPAN + TAIL, 2 * HEAD), bf16),
            pair,
            tail,
            sds((SPAN, 2 * HEAD), f32),
        ),
        in_specs=[VMEM] * 7,
        out_specs=(VMEM,) * 5,
        scratch_shapes=[
            pltpu.VMEM((window, HEAD), bf16),
            pltpu.VMEM((window, HEAD), bf16),
            pltpu.VMEM((HEAD, window), bf16),
            pltpu.VMEM((HEAD, window), bf16),
            pltpu.VMEM((pairs * BLOCK, WIDE), f32),
            pltpu.VMEM((SPAN, WIDE), bf16),
            pltpu.VMEM((pairs * BLOCK, WIDE), bf16),
            pltpu.VMEM((pairs * BLOCK, WIDE), bf16),
            pltpu.VMEM((window, HEAD), f32),
            pltpu.VMEM((window, HEAD), f32),
            pltpu.VMEM((SPAN, WIDE), bf16),
        ],
        cost_estimate=cost(6 * flops, pairs * BLOCK * WIDE),
        compiler_params=params(36),
        name="attention",
    )(grads, queries, starts, own, near, mid, far)

    back = exchanged(dchunks)
    received = core_swapped(dnear_far)
    far_back = passed_along(dfar, -3, (0,))
    merged = pl.pallas_call(
        merge_kernel,
        out_shape=pair,
        in_specs=[VMEM] * 2,
        out_specs=VMEM,
        compiler_params=params(4),
        name="merge",
    )(dmid, received)
    shifted = passed_along(merged, -2)
    folded = pl.pallas_call(
        fold_kernel,
        out_shape=sds((SPAN, 2 * HEAD), f32),
        in_specs=[VMEM] * 3,
        out_specs=VMEM,
        cost_estimate=cost(12 * flops),
        compiler_params=params(4),
        name="fold",
    )(down, received, far_back)
    grad_key, grad_value = pl.pallas_call(
        sum_kernel,
        out_shape=(sds((SPAN, HEAD), bf16),) * 2,
        in_specs=[VMEM] * 2,
        out_specs=(HBM,) * 2,
        scratch_shapes=[pltpu.VMEM((2, SPAN, HEAD), bf16), dma((2,))],
        compiler_params=params(4),
        name="sum",
    )(folded, shifted)
    grad_query = pl.pallas_call(
        place_kernel,
        out_shape=sds((share, parts * WIDE), bf16),
        in_specs=[VMEM],
        out_specs=HBM,
        scratch_shapes=[dma((parts,))],
        compiler_params=params(4),
        name="place",
    )(back)
    return grad_query, grad_key, grad_value


def solution(mesh):
    in_specs = (
        P("ctx", "kvh"),
        P("ctx", "kvh"),
        P("ctx", "kvh"),
        P(("ctx", "kvh"), None),
        P("ctx"),
    )
    out_specs = (P(("ctx", "kvh"), None), P("ctx", "kvh"), P("ctx", "kvh"))
    return jax.shard_map(body, mesh=mesh, in_specs=in_specs, out_specs=out_specs, check_vma=False)
```

```python
import math

import jax
import jax.numpy as jnp
from jax import lax
from jax.experimental import pallas as pl
from jax.experimental.pallas import tpu as pltpu
from jax.sharding import PartitionSpec as P

HEAD = 128
GROUP = 4
BLOCK = 128
OWN = 3
REACH = 9
WINDOW = REACH + OWN - 1
WIDE = GROUP * BLOCK
SPAN = OWN * BLOCK
TAIL = 2 * BLOCK
INV_ROOT = HEAD ** (-0.5)
TO_EXP2 = INV_ROOT * math.log2(math.e)
MIB = 2**20

NT = (((1,), (1,)), ((), ()))
NN = (((1,), (0,)), ((), ()))
VMEM = pl.BlockSpec(memory_space=pltpu.VMEM)
HBM = pl.BlockSpec(memory_space=pltpu.HBM)


def dot(a, b, dims):
    return lax.dot_general(a, b, dims, preferred_element_type=jnp.float32)


def block(index, count=1):
    return slice(index * BLOCK, (index + count) * BLOCK)


def heads_stacked(value):
    return jnp.concatenate([value[:, block(h)] for h in range(GROUP)], axis=0)


def started(pairs, sems):
    copies = [pltpu.make_async_copy(a, b, sems.at[n]) for n, (a, b) in enumerate(pairs)]
    for copy in copies:
        copy.start()
    return copies


def finish(copies):
    for copy in copies:
        copy.wait()


def peer_at(position, parts):
    return lax.rem(position + lax.rem(lax.axis_index("ctx"), 2) * (parts // 4), parts)


def on_odd_core():
    return lax.rem(lax.axis_index("ctx"), 2) == 1


def peer_cols(position, parts):
    return pl.ds(pl.multiple_of(peer_at(position, parts) * WIDE, WIDE), WIDE)


def prepare_kernel(
    start_hbm, query_hbm, grad_hbm, key_hbm, value_hbm,
    chunks, pair, tail, query, starts, start_ref, sems
):
    parts = chunks.shape[0]
    last = slice(SPAN - TAIL, SPAN)
    moves = [(start_hbm, start_ref)]
    moves += [(grad_hbm.at[:, peer_cols(p, parts)], chunks.at[p]) for p in range(parts)]
    moves += [
        (key_hbm, pair.at[:, :HEAD]),
        (value_hbm, pair.at[:, HEAD:]),
        (key_hbm.at[last, :], tail.at[:, :HEAD]),
        (value_hbm.at[last, :], tail.at[:, HEAD:]),
        (query_hbm, query),
    ]
    copies = started(moves, sems)
    finish(copies[:1])
    for i in range(OWN):
        starts[row8(i), :] = jnp.full((8, WIDE), start_ref[i], jnp.int32)
    finish(copies[1:])


def later_kernel(own, later):
    later[...] = own[...]


def window_of(part, far, mid, near, own):
    cols = block(part)
    return jnp.concatenate([far[:, cols], mid[:, cols], near[:, cols], own[:, cols]], axis=0)


def causal_mask():
    key_at = lax.broadcasted_iota(jnp.int32, (BLOCK, WIDE), 0)
    query_at = lax.broadcasted_iota(jnp.int32, (BLOCK, WIDE), 1) & (BLOCK - 1)
    return key_at <= query_at


def first_key():
    return lax.axis_index("ctx") * SPAN - (REACH - 1) * BLOCK


def row8(i):
    return slice(8 * i, 8 * i + 8)


def attention_kernel(
    chunks, query_ref, starts, own, near, mid, far,
    dchunks, dnear_far, dmid, dfar, down,
    key_win, value_win, value_t, key_t, scores, grad_ref, weights, held, dkey, dvalue, dquery
):
    parts, share = chunks.shape[0], chunks.shape[1]

    def share_rows(p):
        return pl.ds(pl.multiple_of(peer_at(p, parts) * share, share), share)

    for p in range(parts):
        grad_ref[share_rows(p), :] = chunks[p]
    keys = window_of(0, far, mid, near, own)
    key_win[...] = keys
    key_t[...] = keys.T
    values = window_of(1, far, mid, near, own)
    value_win[...] = values
    value_t[...] = values.T
    causal = causal_mask()
    first = first_key()
    on_diagonal = lax.broadcasted_iota(jnp.int32, (BLOCK, BLOCK), 0) == lax.broadcasted_iota(
        jnp.int32, (BLOCK, BLOCK), 1
    )
    for i in range(OWN):
        mine = block(i * REACH, REACH)
        queries = heads_stacked(query_ref[block(i), :])
        queries_t = queries.T
        start = starts[8 * i : 8 * i + 1, :]
        best = jnp.full((8, WIDE), -jnp.inf, jnp.float32)
        for j in range(REACH):
            score = dot(key_win[block(i + j), :], queries_t, NN)
            allowed = causal if j == REACH - 1 else first + (i + j) * BLOCK >= start
            score = jnp.where(allowed, score, -jnp.inf)
            scores[block(i * REACH + j), :] = score
            best = jnp.maximum(best, jnp.max(score.reshape(BLOCK // 8, 8, WIDE), axis=0))
        best = jnp.max(best, axis=0, keepdims=True)
        total = jnp.zeros((8, WIDE), jnp.float32)
        for j in range(REACH):
            part = jnp.exp2((scores[block(i * REACH + j), :] - best) * TO_EXP2)
            total = total + jnp.sum(part.reshape(BLOCK // 8, 8, WIDE), axis=0)
            weights[block(i * REACH + j), :] = part.astype(jnp.bfloat16)
        inverse = 1.0 / jnp.sum(total, axis=0, keepdims=True)
        attended = (
            dot(value_t[:, block(i, REACH)], weights[mine, :], NN) * inverse
        ).astype(jnp.bfloat16)
        per_row = jnp.concatenate(
            [jnp.broadcast_to(inverse[:, block(h)], (BLOCK, BLOCK)).T for h in range(GROUP)], axis=0
        )
        grads = (heads_stacked(grad_ref[block(i), :]).astype(jnp.float32) * per_row).astype(
            jnp.bfloat16
        )
        grads_t = grads.T
        deltas = []
        for h in range(GROUP):
            cross = dot(grads[block(h), :], attended[:, block(h)], NN)
            deltas.append(jnp.sum(jnp.where(on_diagonal, cross, 0.0), axis=0, keepdims=True))
        delta = jnp.concatenate(deltas, axis=1)
        for j in range(REACH):
            dweight = dot(value_win[block(i + j), :], grads_t, NN)
            weight = weights[block(i * REACH + j), :].astype(jnp.float32)
            held[block(i * REACH + j), :] = (weight * (dweight - delta)).astype(jnp.bfloat16)
        turned = dot(key_t[:, block(i, REACH)], held[mine, :], NN) * INV_ROOT
        for h in range(GROUP):
            dquery[block(i), block(h)] = turned[:, block(h)].T.astype(jnp.bfloat16)
        value_part = dot(weights[mine, :], grads, NN)
        key_part = dot(held[mine, :], queries, NN)
        fresh = 0 if i == 0 else REACH - 1
        if fresh:
            seen = slice(0, fresh * BLOCK)
            dvalue[block(i, fresh), :] += value_part[seen, :]
            dkey[block(i, fresh), :] += key_part[seen, :]
        rest = slice(fresh * BLOCK, REACH * BLOCK)
        dvalue[block(i + fresh, REACH - fresh), :] = value_part[rest, :]
        dkey[block(i + fresh, REACH - fresh), :] = key_part[rest, :]
    for p in range(parts):
        dchunks[p] = dquery[share_rows(p), :]

    def put(ref, at, lo, count):
        to, span = slice(at, at + count), slice(lo, lo + count)
        ref[to, :HEAD] = (dkey[span, :] * INV_ROOT).astype(ref.dtype)
        ref[to, HEAD:] = dvalue[span, :].astype(ref.dtype)

    put(dnear_far, 0, TAIL + SPAN, SPAN)
    put(dnear_far, SPAN, 0, TAIL)
    put(dfar, 0, 0, TAIL)
    put(dmid, 0, TAIL, SPAN)
    put(down, 0, TAIL + 2 * SPAN, SPAN)


def merge_kernel(dmid, received, merged):
    odd = on_odd_core()
    f32 = jnp.float32

    @pl.when(odd)
    def _():
        merged[...] = (dmid[...].astype(f32) + received[:SPAN, :].astype(f32)).astype(merged.dtype)

    @pl.when(jnp.logical_not(odd))
    def _():
        head, last = slice(0, SPAN - TAIL), slice(SPAN - TAIL, SPAN)
        merged[head, :] = dmid[head, :]
        merged[last, :] = (
            dmid[last, :].astype(f32) + received[SPAN:, :].astype(f32)
        ).astype(merged.dtype)


def fold_kernel(down, received, apart, folded):
    odd = on_odd_core()
    f32 = jnp.float32

    @pl.when(odd)
    def _():
        head, last = slice(0, SPAN - TAIL), slice(SPAN - TAIL, SPAN)
        folded[head, :] = down[head, :]
        folded[last, :] = down[last, :] + apart[...].astype(f32)

    @pl.when(jnp.logical_not(odd))
    def _():
        folded[...] = down[...] + received[:SPAN, :].astype(f32)


def sum_kernel(folded, shifted, key_hbm, value_hbm, out, sems):
    total = folded[...] + shifted[...].astype(jnp.float32)
    for part in range(2):
        out[part] = total[:, block(part)].astype(out.dtype)
    finish(started([(out.at[0], key_hbm), (out.at[1], value_hbm)], sems))


def place_kernel(chunks, out_hbm, sems):
    parts = chunks.shape[0]
    finish(
        started([(chunks.at[p], out_hbm.at[:, peer_cols(p, parts)]) for p in range(parts)], sems)
    )


def passed_along(value, by, parities=(0, 1)):
    length = lax.axis_size("ctx")
    pairs = [
        (i, i + by) for i in range(length) if 0 <= i + by < length and i % 2 in parities
    ]
    return lax.ppermute(value, "ctx", pairs)


def core_swapped(value):
    return lax.ppermute(value, "ctx", [(i, i ^ 1) for i in range(lax.axis_size("ctx"))])


def pinned(*arrays):
    return [pltpu.with_memory_space_constraint(x, pltpu.HBM) for x in arrays]


def cost(flops, exps=0):
    return pl.CostEstimate(flops=int(flops), bytes_accessed=8 * MIB, transcendentals=int(exps))


def params(mib):
    return pltpu.CompilerParams(vmem_limit_bytes=mib * MIB)


def body(query_states, key_states, value_states, grad_output, doc_start):
    parts, length = lax.axis_size("kvh"), lax.axis_size("ctx")
    share = SPAN // parts
    bf16, f32 = jnp.bfloat16, jnp.float32
    sds = jax.ShapeDtypeStruct
    dma = pltpu.SemaphoreType.DMA
    window = WINDOW * BLOCK
    pairs = OWN * REACH
    flops = 2 * pairs * BLOCK * BLOCK * WIDE
    chunked = sds((parts, share, WIDE), bf16)
    pair = sds((SPAN, 2 * HEAD), bf16)
    tail = sds((TAIL, 2 * HEAD), bf16)
    rings = [
        [c * parts + (p + (c % 2) * (parts // 4)) % parts for p in range(parts)]
        for c in range(length)
    ]

    def exchanged(value):
        return lax.all_to_all(
            value, ("ctx", "kvh"), split_axis=0, concat_axis=0, axis_index_groups=rings, tiled=True
        )

    chunks, own, last, queries, starts = pl.pallas_call(
        prepare_kernel,
        out_shape=(
            chunked, pair, tail, sds((SPAN, WIDE), bf16), sds((8 * OWN, WIDE), jnp.int32)
        ),
        in_specs=[HBM] * 5,
        out_specs=(VMEM,) * 5,
        scratch_shapes=[pltpu.SMEM(doc_start.shape, jnp.int32), dma((parts + 6,))],
        compiler_params=params(4),
        name="prepare",
    )(*pinned(doc_start, query_states, grad_output, key_states, value_states))
    grads = exchanged(chunks)
    far = passed_along(last, 3)
    own = pl.pallas_call(
        later_kernel,
        out_shape=pair,
        in_specs=[VMEM],
        out_specs=VMEM,
        cost_estimate=cost(12 * flops),
        compiler_params=params(4),
        name="later",
    )(own)
    mid = passed_along(own, 2)
    near = passed_along(own, 1)

    dchunks, dnear_far, dmid, dfar, down = pl.pallas_call(
        attention_kernel,
        out_shape=(
            chunked,
            sds((SPAN + TAIL, 2 * HEAD), bf16),
            pair,
            tail,
            sds((SPAN, 2 * HEAD), f32),
        ),
        in_specs=[VMEM] * 7,
        out_specs=(VMEM,) * 5,
        scratch_shapes=[
            pltpu.VMEM((window, HEAD), bf16),
            pltpu.VMEM((window, HEAD), bf16),
            pltpu.VMEM((HEAD, window), bf16),
            pltpu.VMEM((HEAD, window), bf16),
            pltpu.VMEM((pairs * BLOCK, WIDE), f32),
            pltpu.VMEM((SPAN, WIDE), bf16),
            pltpu.VMEM((pairs * BLOCK, WIDE), bf16),
            pltpu.VMEM((pairs * BLOCK, WIDE), bf16),
            pltpu.VMEM((window, HEAD), f32),
            pltpu.VMEM((window, HEAD), f32),
            pltpu.VMEM((SPAN, WIDE), bf16),
        ],
        cost_estimate=cost(6 * flops, pairs * BLOCK * WIDE),
        compiler_params=params(36),
        name="attention",
    )(grads, queries, starts, own, near, mid, far)

    back = exchanged(dchunks)
    received = core_swapped(dnear_far)
    far_back = passed_along(dfar, -3, (0,))
    merged = pl.pallas_call(
        merge_kernel,
        out_shape=pair,
        in_specs=[VMEM] * 2,
        out_specs=VMEM,
        compiler_params=params(4),
        name="merge",
    )(dmid, received)
    shifted = passed_along(merged, -2)
    folded = pl.pallas_call(
        fold_kernel,
        out_shape=sds((SPAN, 2 * HEAD), f32),
        in_specs=[VMEM] * 3,
        out_specs=VMEM,
        cost_estimate=cost(12 * flops),
        compiler_params=params(4),
        name="fold",
    )(down, received, far_back)
    grad_key, grad_value = pl.pallas_call(
        sum_kernel,
        out_shape=(sds((SPAN, HEAD), bf16),) * 2,
        in_specs=[VMEM] * 2,
        out_specs=(HBM,) * 2,
        scratch_shapes=[pltpu.VMEM((2, SPAN, HEAD), bf16), dma((2,))],
        compiler_params=params(4),
        name="sum",
    )(folded, shifted)
    grad_query = pl.pallas_call(
        place_kernel,
        out_shape=sds((share, parts * WIDE), bf16),
        in_specs=[VMEM],
        out_specs=HBM,
        scratch_shapes=[dma((parts,))],
        compiler_params=params(4),
        name="place",
    )(back)
    return grad_query, grad_key, grad_value


def solution(mesh):
    in_specs = (
        P("ctx", "kvh"),
        P("ctx", "kvh"),
        P("ctx", "kvh"),
        P(("ctx", "kvh"), None),
        P("ctx"),
    )
    out_specs = (P(("ctx", "kvh"), None), P("ctx", "kvh"), P("ctx", "kvh"))
    return jax.shard_map(body, mesh=mesh, in_specs=in_specs, out_specs=out_specs, check_vma=False)
```
